256 devices in a mesh: inst: 4 (over x), section: 8 (over z_lo, core), tp: 8 (over y, z_hi).
Axes of the slice: x: 4, y: 4, z: 8 (z_hi: 2, z_lo: 4; z = z_hi * 4 + z_lo), core: 2. Of those that a mesh axis runs over, the one named last changes fastest.
Arguments:
- hidden: bfloat16 [64, 8192], P('inst', 'tp'), may hold values from -6 to 6
- queries: bfloat16 [8, 64, 4096], P('section', 'inst', 'tp'), may hold values from -32 to 32
- new_kv: bfloat16 [8, 64, 2048], P('section', 'inst', 'tp'), may hold values from -12 to 12
- kv_cache: bfloat16 [8, 64, 8, 512, 256], P('section', 'inst', 'tp'), may hold values from -64 to 64
- lengths: int32 [64], P('inst'), may hold values from 1 to 512, as said below
- anchor: int32 [64], replicated, may hold values from 0 to 63, as said below
- out_weight: bfloat16 [8, 4096, 8192], P('section', 'tp'), may hold values from -0.09375 to 0.09375
Outputs:
- layer_outputs: bfloat16 [8, 64, 8192], P('section', 'inst', 'tp')
- moved_cache: bfloat16 [8, 64, 8, 512, 256], P('section', 'inst', 'tp')
- moved_len: int32 [64], P('inst')
The draws below stay inside these ranges and needn't reach their ends.
Inputs may be any that keep to these rules, and one draw needn't show every extreme that they name: anchor is a permutation of all 64 slots; each instance receives exactly 2 requests from each other instance and keeps the rest of its own. `lengths`: some request has exactly 512 positions.
All inputs are finite; a program needn't handle non-finite values.
Results may differ from the reference program's by a relative error of at most 0.0095.
Values may be sent and summed in bfloat16 or wider, within the bound.
A program may use at most 128 MiB of HBM per device.

```python
import math
import jax
import jax.numpy as jnp
from jax import lax

D = 8192
KVH = 8
HEADS = 32
HD = 128
SLOTS = 16
CTX = 512
MIG = 2
LAYERS = 8
N_INST = 4


def draw_kv_cache(key, part):
    key = jax.random.fold_in(key, 11)
    noise = jnp.clip(jax.random.normal(key, (LAYERS, N_INST * SLOTS, KVH, CTX, 2 * HD), jnp.float32), -6.0, 6.0)
    return noise.astype(jnp.bfloat16)


def draw_queries(key, part):
    key = jax.random.fold_in(key, 12)
    noise = jnp.clip(jax.random.normal(key, (LAYERS, N_INST * SLOTS, HEADS, HD), jnp.float32), -6.0, 6.0)
    return noise.reshape(LAYERS, N_INST * SLOTS, HEADS * HD).astype(jnp.bfloat16)


def draw_lengths(key, part):
    key = jax.random.fold_in(key, 13)
    first = jax.random.randint(jax.random.fold_in(key, 1), (N_INST * SLOTS,), 1, CTX + 1)
    second = jax.random.randint(jax.random.fold_in(key, 2), (N_INST * SLOTS,), 1, CTX + 1)
    spans = jnp.minimum(first, second)
    chosen = jax.random.randint(jax.random.fold_in(key, 3), (), 0, N_INST * SLOTS)
    return spans.at[chosen].set(CTX).astype(jnp.int32)


def draw_anchor(key, part):
    key = jax.random.fold_in(key, 21)
    kept = SLOTS - (N_INST - 1) * MIG
    orders = [source * SLOTS + jax.random.permutation(jax.random.fold_in(key, source), SLOTS) for source in range(N_INST)]
    dest_rows = []
    for target in range(N_INST):
        pieces = [orders[target][:kept]]
        for source in range(N_INST):
            if source != target:
                offset = target if target < source else target - 1
                pieces.append(orders[source][kept + MIG * offset:kept + MIG * (offset + 1)])
        joined = jnp.concatenate(pieces)
        dest_rows.append(jax.random.permutation(jax.random.fold_in(key, 100 + target), joined))
    return jnp.concatenate(dest_rows).astype(jnp.int32)


def block_levels(own_key, shape, shards, smallest, largest):
    loudness = 1.0
    for position, blocks in shards:
        steps = jax.random.uniform(jax.random.fold_in(jax.random.fold_in(own_key, 6), position), (blocks,), jnp.float32, smallest / len(shards), largest / len(shards))
        loudness = loudness * jnp.repeat(jnp.exp(steps), shape[position] // blocks).reshape((-1,) + (1,) * (len(shape) - 1 - position))
    return loudness


def gaussian(rng, extent, scale, limit, cuts=(), kind=jnp.bfloat16):
    entries = scale * jax.random.normal(rng, extent, jnp.float32)
    if cuts:
        entries = entries * block_levels(rng, extent, cuts, -0.22, 0.18)
    return jnp.clip(entries, -limit, limit).astype(kind)


def setup_inputs(seed: int = 0) -> dict:
    keys = jax.random.split(jax.random.key(seed), 8)
    hidden = gaussian(keys[0], (N_INST * SLOTS, D), 1.0, 6.0, ((0, 4), (1, 8)))
    queries = draw_queries(jax.random.fold_in(keys[7], 71), 0)
    new_kv = gaussian(keys[2], (LAYERS, N_INST * SLOTS, KVH * 2 * HD), 2.5, 12.0, ((0, 8), (1, 4), (2, 8)))
    kv_cache = draw_kv_cache(jax.random.fold_in(keys[7], 71), 0)
    lengths = draw_lengths(jax.random.fold_in(keys[7], 71), 0)
    anchor = draw_anchor(jax.random.fold_in(keys[7], 71), 0)
    out_weight = gaussian(keys[6], (LAYERS, HEADS * HD, D), (HEADS * HD) ** -0.5, 0.09375, ((0, 8), (1, 8)))
    return {"hidden": hidden, "queries": queries, "new_kv": new_kv, "kv_cache": kv_cache, "lengths": lengths, "anchor": anchor, "out_weight": out_weight}


def attend(query, new_pair, key_part, value_part, live_len):
    head_dim = query.shape[-1]
    inv_root = 1.0 / math.sqrt(head_dim)
    scores = jnp.einsum('rkqd,rkpd->rkqp', query, key_part) * inv_root
    positions = jnp.arange(key_part.shape[2], dtype=jnp.int32)
    live = positions[None, None, None, :] < live_len[:, None, None, None]
    scores = jnp.where(live, scores, -jnp.inf)
    new_score = jnp.einsum('rkqd,rkd->rkq', query, new_pair[..., :head_dim]) * inv_root
    row_max = jnp.maximum(lax.optimization_barrier(jnp.max(scores, axis=-1)), new_score)
    expo = jnp.exp(scores - row_max[..., None])
    new_expo = jnp.exp(new_score - row_max)
    summed = lax.optimization_barrier(jnp.sum(expo, axis=-1)) + new_expo
    probs = (expo / summed[..., None]).astype(jnp.bfloat16)
    new_prob = (new_expo / summed).astype(jnp.bfloat16)
    result = jnp.einsum('rkqp,rkpd->rkqd', probs.astype(jnp.float32), value_part)
    result = result + new_prob.astype(jnp.float32)[..., None] * new_pair[:, :, None, head_dim:]
    return result.astype(jnp.bfloat16).reshape(query.shape[0], -1)

def reference(hidden, queries, new_kv, kv_cache, lengths, anchor, out_weight):
    slot_total = N_INST * SLOTS
    moved_len = lengths[anchor]
    moved_cache = kv_cache[:, anchor]

    def one_layer(layer_args):
        query_rows, pair_rows, cache_rows, weight = layer_args
        moved = cache_rows.astype(jnp.float32)
        query = query_rows.astype(jnp.float32).reshape(slot_total, KVH, HEADS // KVH, HD)
        new_pair = pair_rows.astype(jnp.float32).reshape(slot_total, KVH, 2 * HD)
        attended = attend(query, new_pair, moved[..., :HD], moved[..., HD:], moved_len)
        return jnp.dot(attended, weight, preferred_element_type=jnp.float32)
    deltas = lax.map(one_layer, (queries, new_kv, moved_cache, out_weight))
    summed = hidden.astype(jnp.float32)[None] + jnp.cumsum(deltas, axis=0)
    return (summed.astype(jnp.bfloat16), moved_cache, moved_len.astype(jnp.int32))
```

```python
import functools
import math

import jax
import jax.numpy as jnp
from jax import lax
from jax.experimental import pallas as pl
from jax.experimental.pallas import tpu as pltpu
from jax.sharding import PartitionSpec as P

MESH = pl.DeviceIdType.MESH
BF = jnp.bfloat16
F32 = jnp.float32
I32 = jnp.int32

INST = 4
TP = 8
SECTIONS = 8
SLOTS = 16
MIG = 2
GROUP = 4
HD = 128
CTX = 512
MODEL = 8192
COLS = MODEL // TP
FIRST = 256
SHIFTS = (1, 2, 3)
MOVES = len(SHIFTS) * MIG
ORDER = (3, 5, 1, 7, 4, 2, 6)
INV_ROOT = 1.0 / math.sqrt(HD)

AT_DEST = 0
AT_LEN = 8
AT_SLOT = 16
AT_POS = 32
INFO = 48


def wrap(value, count):
    return lax.rem(value + count, count)


def attend_slot(query, keys, values, length, first_len=None):
    rows = query.astype(BF)
    parts = [
        lax.dot_general(rows, block, (((1,), (1,)), ((), ())), preferred_element_type=F32) for block in keys
    ]
    scores = (parts[0] if len(parts) == 1 else jnp.concatenate(parts, axis=1)) * INV_ROOT
    new_key, new_value = query[4:5, :], query[5:6, :]
    new_score = jnp.sum(query * new_key, axis=1, keepdims=True) * INV_ROOT
    place = lax.broadcasted_iota(I32, scores.shape, 1)
    scores = jnp.where(place < length, scores, -jnp.inf)
    top = jnp.maximum(jnp.max(scores, axis=1, keepdims=True), new_score)
    expo = jnp.exp(scores - top)
    new_expo = jnp.exp(new_score - top)
    total = jnp.sum(expo, axis=1, keepdims=True) + new_expo
    probs = (expo / total).astype(BF)
    new_prob = (new_expo / total).astype(BF).astype(F32)
    result = new_prob * new_value
    start = 0
    for block in values:
        stop = start + block.shape[0]
        result = result + jnp.dot(probs[:, start:stop], block, preferred_element_type=F32)
        start = stop
    return result


def gather_kernel(anchor, lengths, q_ref, new_ref, kv, q_slots, s1, s2, s3, a1, a2, a3, b1, b2, b3, info, sems):
    me = lax.axis_index("inst")
    first, second = (a1, a2, a3), (b1, b2, b3)
    copies = []
    for at, shift in enumerate(SHIFTS):
        dest = wrap(me + shift, INST)
        count = jnp.int32(0)
        picked = [jnp.int32(0)] * MIG
        for slot in range(SLOTS):
            source = anchor[dest * SLOTS + slot]
            hit = lax.shift_right_logical(source, 4) == me
            for rank in range(MIG):
                picked[rank] = jnp.where(hit & (count == rank), source & (SLOTS - 1), picked[rank])
            count = count + hit.astype(I32)
        for rank in range(MIG):
            one = at * MIG + rank
            info[AT_LEN + one] = lengths[picked[rank]]
            for part, (refs, begin, size) in enumerate(((first, 0, FIRST), (second, FIRST, CTX - FIRST))):
                copy = pltpu.make_async_copy(
                    kv.at[0, picked[rank], 0, pl.ds(begin, size)], refs[at].at[rank], sems.at[part, one]
                )
                copy.start()
                copies.append(copy)
    queries = q_ref[0].astype(F32)
    pairs = new_ref[0].astype(F32)
    for head in range(GROUP):
        q_slots[:, head, :] = queries[:, head * HD : (head + 1) * HD]
    q_slots[:, 4, :] = pairs[:, :HD]
    q_slots[:, 5, :] = pairs[:, HD:]
    q_slots[:, 6, :] = jnp.zeros((SLOTS, HD), F32)
    q_slots[:, 7, :] = jnp.zeros((SLOTS, HD), F32)
    counts = [jnp.int32(0)] * len(SHIFTS)
    found = [jnp.int32(0)] * MOVES
    for slot in range(SLOTS):
        source = anchor[me * SLOTS + slot]
        owner = lax.shift_right_logical(source, 4)
        position = jnp.int32(-1)
        for at, shift in enumerate(SHIFTS):
            hit = owner == wrap(me - shift, INST)
            position = jnp.where(hit, at * MIG + counts[at], position)
            for rank in range(MIG):
                one = at * MIG + rank
                found[one] = jnp.where(hit & (counts[at] == rank), slot, found[one])
            counts[at] = counts[at] + hit.astype(I32)
        info[AT_SLOT + slot] = source & (SLOTS - 1)
        info[AT_POS + slot] = position
    for at, out in enumerate((s1, s2, s3)):
        for rank in range(MIG):
            info[AT_DEST + at * MIG + rank] = found[at * MIG + rank]
        out[...] = jnp.concatenate([q_slots[found[at * MIG + rank]] for rank in range(MIG)], axis=0).astype(BF)
    for spare in (AT_DEST + 6, AT_DEST + 7, AT_LEN + 6, AT_LEN + 7):
        info[spare] = jnp.int32(0)
    for copy in copies:
        copy.wait()


def local_kernel(info, lengths, q_slots, kv, moved, attended, cache, result, read_sems, write_sems):
    def is_local(slot):
        return info[AT_POS + slot] < 0

    def read(slot):
        return pltpu.make_async_copy(kv.at[0, info[AT_SLOT + slot], 0], cache.at[slot], read_sems.at[slot])

    def write(slot):
        return pltpu.make_async_copy(cache.at[slot], moved.at[0, slot, 0], write_sems.at[slot])

    for slot in range(SLOTS):
        pl.when(is_local(slot))(lambda slot=slot: read(slot).start())
    result[...] = jnp.zeros_like(result)
    for slot in range(SLOTS):

        @pl.when(is_local(slot))
        def _(slot=slot):
            read(slot).wait()
            write(slot).start()
            length = lengths[info[AT_SLOT + slot]]
            result[slot] = attend_slot(
                q_slots[slot], [cache[slot, :, :HD]], [cache[slot, :, HD:]], length
            )

    attended[...] = jnp.concatenate([result[:, head, :] for head in range(GROUP)], axis=1).astype(BF)
    for slot in range(SLOTS):
        pl.when(is_local(slot))(lambda slot=slot: write(slot).wait())


def chain_kernel(
    info, lengths, q1, q2, q3, a1, a2, a3, b1, b2, b3, attended, hidden, weight,
    c1, c2, c3, out, moved_len,
    w_blocks, send_l, recv_l, send_m, recv_m, delta_l, part_l, delta_m, part_m,
    back, back_in, tile, tile_in, rows_m, rows, acc_m,
    w_sems, back_sems, tile_sems, bulk_sems, l_sems, m_sems, pl_sems, pm_sems,
):
    inst, section, tp = (lax.axis_index(name) for name in ("inst", "section", "tp"))
    queries, first, second, arrived = (q1, q2, q3), (a1, a2, a3), (b1, b2, b3), (c1, c2, c3)

    def on_inst(shift):
        return {"inst": wrap(inst + shift, INST)}

    def on_tp(distance):
        return {"tp": wrap(tp + distance, TP)}

    def remote(source, target, sems, at, device):
        return pltpu.make_async_remote_copy(
            src_ref=source, dst_ref=target, send_sem=sems.at[0, at], recv_sem=sems.at[1, at],
            device_id=device, device_id_type=MESH,
        )

    barrier = pltpu.get_barrier_semaphore()
    for shift in SHIFTS:
        pl.semaphore_signal(barrier, inc=1, device_id=on_inst(shift), device_id_type=MESH)
    for distance in ORDER:
        pl.semaphore_signal(barrier, inc=1, device_id=on_tp(distance), device_id_type=MESH)
    for distance in range(1, SECTIONS):

        @pl.when(section >= distance)
        def _(distance=distance):
            pl.semaphore_signal(barrier, inc=1, device_id={"section": section - distance}, device_id_type=MESH)

    loads = {}
    for distance in ORDER + (0,):
        columns = pl.ds(pl.multiple_of(wrap(tp + distance, TP) * COLS, COLS), COLS)
        loads[distance] = pltpu.make_async_copy(
            weight.at[0, :, columns], w_blocks.at[distance], w_sems.at[distance]
        )
        loads[distance].start()

    for at in range(len(SHIFTS)):
        both = queries[at][...].astype(F32)
        results = []
        for rank in range(MIG):
            results.append(
                attend_slot(
                    both[rank * 8 : rank * 8 + 8, :],
                    [first[at][rank, :, :HD], second[at][rank, :, :HD]],
                    [first[at][rank, :, HD:], second[at][rank, :, HD:]],
                    info[AT_LEN + at * MIG + rank],
                )
            )
        back[at] = jnp.concatenate(results, axis=0).astype(BF)
    lane = lax.broadcasted_iota(I32, (8, 128), 1)
    for at in range(len(SHIFTS)):
        filled = jnp.zeros((8, 128), I32)
        for rank in range(MIG):
            filled = jnp.where(lane == rank, info[AT_LEN + at * MIG + rank], filled)
        tile[at] = filled

    pl.semaphore_wait(barrier, len(SHIFTS) + TP - 1 + SECTIONS - 1 - section)

    back_copies, tile_copies, bulk_copies = [], [], []
    for at, shift in enumerate(SHIFTS):
        back_copies.append(remote(back.at[at], back_in.at[at], back_sems, at, on_inst(shift)))
        tile_copies.append(remote(tile.at[at], tile_in.at[at], tile_sems, at, on_inst(shift)))
        bulk_copies.append(remote(second[at], arrived[at], bulk_sems, at, on_inst(shift)))
    for copy in back_copies + tile_copies:
        copy.start()
    for copy in (bulk_copies[1], bulk_copies[0], bulk_copies[2]):
        copy.start()

    stay = attended[...]
    stay_copies = {}
    own_l = None
    for distance in ORDER + (0,):
        loads[distance].wait()
        share = jnp.dot(stay, w_blocks[distance], preferred_element_type=F32)
        if distance == 0:
            own_l = share
        else:
            send_l[distance] = share.astype(BF)
            copy = remote(send_l.at[distance], recv_l.at[distance], l_sems, distance, on_tp(distance))
            copy.start()
            stay_copies[distance] = copy

    for copy in back_copies:
        copy.wait_recv()
    for at in range(len(SHIFTS)):
        both = back_in[at].astype(F32)
        for rank in range(MIG):
            rows_m[at * MIG + rank] = both[rank * 8 : rank * 8 + 8, :]
    rows_m[6] = jnp.zeros((8, HD), F32)
    rows_m[7] = jnp.zeros((8, HD), F32)
    come = jnp.concatenate([rows_m[:, head, :] for head in range(GROUP)], axis=1).astype(BF)
    half = COLS // 2
    come_copies = {}
    own_m = None
    for distance in ORDER + (0,):
        share = jnp.dot(come, w_blocks[distance], preferred_element_type=F32)
        share = jnp.concatenate([share[:, :half], share[:, half:]], axis=0)
        if distance == 0:
            own_m = share
        else:
            send_m[distance] = share.astype(BF)
            copy = remote(send_m.at[distance], recv_m.at[distance], m_sems, distance, on_tp(distance))
            copy.start()
            come_copies[distance] = copy

    def later(group, source, target, sems, do):
        for distance in range(1, SECTIONS):

            @pl.when(section + distance < SECTIONS)
            def _(distance=distance):
                do(remote(source, target.at[distance], sems, distance, {"section": section + distance}))

    def start(copy):
        copy.start()

    def sent(copy):
        copy.wait_send()

    total = own_l
    for distance in ORDER:
        stay_copies[distance].wait_recv()
        total = total + recv_l[distance].astype(F32)
    delta_l[...] = total.astype(BF)
    later("stay", delta_l, part_l, pl_sems, start)
    rows[...] = hidden[...].astype(F32) + total
    total = own_m
    for distance in ORDER:
        come_copies[distance].wait_recv()
        total = total + recv_m[distance].astype(F32)
    delta_m[...] = total.astype(BF)
    later("come", delta_m, part_m, pm_sems, start)
    acc_m[...] = total

    for copy in tile_copies:
        copy.wait_recv()
    lens = jnp.zeros((8, 128), I32)
    for slot in range(SLOTS):
        lens = jnp.where(lane == slot, lengths[info[AT_SLOT + slot]], lens)
    for at in range(len(SHIFTS)):
        for rank in range(MIG):
            value = jnp.sum(jnp.where(lane == rank, tile_in[at], 0), axis=1, keepdims=True)
            lens = jnp.where(lane == info[AT_DEST + at * MIG + rank], value, lens)
    moved_len[...] = lens

    for distance in range(1, SECTIONS):

        @pl.when(section >= distance)
        def _(distance=distance):
            remote(delta_l, part_l.at[distance], pl_sems, distance, {"section": section}).wait_recv()
            rows[...] += part_l[distance].astype(F32)

    for distance in range(1, SECTIONS):

        @pl.when(section >= distance)
        def _(distance=distance):
            remote(delta_m, part_m.at[distance], pm_sems, distance, {"section": section}).wait_recv()
            acc_m[...] += part_m[distance].astype(F32)

    low, high = acc_m.at[pl.ds(0, 8)], acc_m.at[pl.ds(8, 8)]
    for slot in range(SLOTS):
        position = info[AT_POS + slot]
        place = jnp.maximum(position, 0)
        for part, ref in enumerate((low, high)):
            extra = jnp.where(position >= 0, ref[pl.ds(place, 1), :], 0.0)
            rows[slot : slot + 1, part * half : (part + 1) * half] += extra
    out[...] = rows[...].astype(BF)

    later("stay", delta_l, part_l, pl_sems, sent)
    later("come", delta_m, part_m, pm_sems, sent)
    for copy in list(stay_copies.values()) + list(come_copies.values()) + back_copies + tile_copies:
        copy.wait_send()
    for copy in bulk_copies:
        copy.wait()


def place_kernel(info, a1, a2, a3, c1, c2, c3, out_rows, lens, moved_in, moved, out, moved_len, scalars, sems, more):
    del moved_in
    copies = [
        pltpu.make_async_copy(out_rows, out.at[0], more.at[0]),
        pltpu.make_async_copy(lens, scalars, more.at[1]),
    ]
    for at, (early, late) in enumerate(zip((a1, a2, a3), (c1, c2, c3))):
        for rank in range(MIG):
            one = at * MIG + rank
            target = moved.at[0, info[AT_DEST + one], 0]
            copies.append(
                pltpu.make_async_copy(early.at[rank], target.at[pl.ds(0, FIRST)], sems.at[0, one])
            )
            copies.append(
                pltpu.make_async_copy(late.at[rank], target.at[pl.ds(FIRST, CTX - FIRST)], sems.at[1, one])
            )
    for copy in copies:
        copy.start()
    copies[1].wait()
    for slot in range(SLOTS):
        moved_len[slot] = scalars[0, slot]
    for copy in copies[:1] + copies[2:]:
        copy.wait()


def specs(*spaces):
    return [pl.BlockSpec(memory_space=space) for space in spaces]


def body(hidden, queries, new_kv, kv_cache, lengths, anchor, out_weight):
    vmem, smem, hbm = pltpu.VMEM, pltpu.SMEM, pltpu.HBM
    dma = pltpu.SemaphoreType.DMA
    rest = CTX - FIRST
    early = [vmem((MIG, FIRST, 2 * HD), BF)] * 3
    late = [vmem((MIG, rest, 2 * HD), BF)] * 3
    gathered = pl.pallas_call(
        gather_kernel,
        out_shape=[vmem((SLOTS, 8, HD), F32)] + [vmem((16, HD), BF)] * 3 + early + late
        + [jax.ShapeDtypeStruct((INFO,), I32)],
        in_specs=specs(smem, smem, vmem, vmem, hbm),
        out_specs=specs(*[vmem] * 10, smem),
        scratch_shapes=[dma((2, MOVES))],
        compiler_params=pltpu.CompilerParams(vmem_limit_bytes=8 << 20),
        name="gather",
    )(anchor, lengths, queries, new_kv, kv_cache)
    q_slots, asked, first, second, info = gathered[0], gathered[1:4], gathered[4:7], gathered[7:10], gathered[10]

    def permute(value, shift):
        return lax.ppermute(value, "inst", [(i, (i + shift) % INST) for i in range(INST)])

    asked = [permute(value, -shift) for value, shift in zip(asked, SHIFTS)]
    first_in = [permute(value, shift) for value, shift in zip(first, SHIFTS)]
    moved, attended = pl.pallas_call(
        local_kernel,
        out_shape=[jax.ShapeDtypeStruct(kv_cache.shape, BF), vmem((SLOTS, GROUP * HD), BF)],
        in_specs=specs(smem, smem, vmem, hbm),
        out_specs=specs(hbm, vmem),
        scratch_shapes=[
            vmem((SLOTS, CTX, 2 * HD), BF), vmem((SLOTS, 8, HD), F32), dma((SLOTS,)), dma((SLOTS,)),
        ],
        compiler_params=pltpu.CompilerParams(vmem_limit_bytes=12 << 20),
        name="local",
    )(info, lengths, q_slots, kv_cache)
    arrived = pl.pallas_call(
        chain_kernel,
        out_shape=late + [vmem((SLOTS, COLS), BF), vmem((8, 128), I32)],
        in_specs=specs(smem, smem, *[vmem] * 11, hbm),
        out_specs=specs(*[vmem] * 5),
        scratch_shapes=[
            vmem((TP, GROUP * HD, COLS), BF),
            vmem((TP, 16, COLS), BF), vmem((TP, 16, COLS), BF),
            vmem((TP, 16, COLS // 2), BF), vmem((TP, 16, COLS // 2), BF),
            vmem((16, COLS), BF), vmem((SECTIONS, 16, COLS), BF),
            vmem((16, COLS // 2), BF), vmem((SECTIONS, 16, COLS // 2), BF),
            vmem((3, 16, HD), BF), vmem((3, 16, HD), BF),
            vmem((3, 8, 128), I32), vmem((3, 8, 128), I32),
            vmem((8, 8, HD), F32), vmem((SLOTS, COLS), F32), vmem((16, COLS // 2), F32),
            dma((TP,)), dma((2, 3)), dma((2, 3)), dma((2, 3)),
            dma((2, TP)), dma((2, TP)), dma((2, SECTIONS)), dma((2, SECTIONS)),
        ],
        compiler_params=pltpu.CompilerParams(
            collective_id=0, has_side_effects=True, vmem_limit_bytes=24 << 20
        ),
        name="chain",
    )(info, lengths, *asked, *first, *second, attended, hidden, out_weight)
    second_in, out_rows, lens = arrived[:3], arrived[3], arrived[4]
    moved, out, moved_len = pl.pallas_call(
        place_kernel,
        out_shape=[
            jax.ShapeDtypeStruct(kv_cache.shape, BF),
            jax.ShapeDtypeStruct((1, SLOTS, COLS), BF),
            jax.ShapeDtypeStruct((SLOTS,), I32),
        ],
        in_specs=specs(smem, *[vmem] * 8, hbm),
        out_specs=specs(hbm, hbm, smem),
        scratch_shapes=[pltpu.SMEM((8, 128), I32), dma((2, MOVES)), dma((2,))],
        input_output_aliases={9: 0},
        compiler_params=pltpu.CompilerParams(vmem_limit_bytes=8 << 20),
        name="place",
    )(info, *first_in, *second_in, out_rows, lens, moved)
    return out, moved, moved_len


def solution(mesh):
    return jax.shard_map(
        body,
        mesh=mesh,
        in_specs=(
            P("inst", "tp"),
            P("section", "inst", "tp"),
            P("section", "inst", "tp"),
            P("section", "inst", "tp", None, None),
            P("inst"),
            P(),
            P("section", "tp", None),
        ),
        out_specs=(P("section", "inst", "tp"), P("section", "inst", "tp", None, None), P("inst")),
        check_vma=False,
    )
```

```python
import functools
import math

import jax
import jax.numpy as jnp
from jax import lax
from jax.experimental import pallas as pl
from jax.experimental.pallas import tpu as pltpu
from jax.sharding import PartitionSpec as P

MESH = pl.DeviceIdType.MESH
BF = jnp.bfloat16
F32 = jnp.float32
I32 = jnp.int32

INST = 4
TP = 8
SECTIONS = 8
SLOTS = 16
MIG = 2
GROUP = 4
HD = 128
CTX = 512
MODEL = 8192
COLS = MODEL // TP
CUT = 128
EARLY = 96
LATE = CTX - EARLY
SHIFTS = (1, 2, 3)
MOVES = len(SHIFTS) * MIG
STAY = SLOTS - MOVES
ORDER = (3, 5, 1, 7, 4, 2, 6)
INV_ROOT = 1.0 / math.sqrt(HD)

def wrap(value, count):
    return lax.rem(value + count, count)


def attend(queries, keys, values, lengths):
    scores = []
    for query, blocks in zip(queries, keys):
        rows = query.astype(BF)
        parts = [
            lax.dot_general(rows, block, (((1,), (1,)), ((), ())), preferred_element_type=F32) for block in blocks
        ]
        scores.append(jnp.concatenate(parts, axis=1))
    place = lax.broadcasted_iota(I32, (8, CTX), 1)
    probs = []
    for query, score, length in zip(queries, scores, lengths):
        score = jnp.where(place < length, score * INV_ROOT, -jnp.inf)
        new_score = jnp.sum(query * query[4:5, :], axis=1, keepdims=True) * INV_ROOT
        top = jnp.maximum(jnp.max(score, axis=1, keepdims=True), new_score)
        expo = jnp.exp(score - top)
        new_expo = jnp.exp(new_score - top)
        scale = 1.0 / (jnp.sum(expo, axis=1, keepdims=True) + new_expo)
        probs.append(((expo * scale).astype(BF), (new_expo * scale).astype(BF).astype(F32)))
    results = []
    for query, (prob, new_prob), blocks in zip(queries, probs, values):
        result = new_prob * query[5:6, :]
        start = 0
        for block in blocks:
            stop = start + block.shape[0]
            result = result + jnp.dot(prob[:, start:stop], block, preferred_element_type=F32)
            start = stop
        results.append(result)
    return results


def scan_leaving(anchor, me, shift):
    dest = wrap(me + shift, INST)
    count = jnp.int32(0)
    picked = [jnp.int32(0)] * MIG
    for slot in range(SLOTS):
        source = anchor[dest * SLOTS + slot]
        hit = lax.shift_right_logical(source, 4) == me
        for rank in range(MIG):
            picked[rank] = jnp.where(hit & (count == rank), source & (SLOTS - 1), picked[rank])
        count = count + hit.astype(I32)
    return picked


def scan_arriving(anchor, me):
    counts = [jnp.int32(0)] * len(SHIFTS)
    found = [jnp.int32(0)] * MOVES
    positions = []
    for slot in range(SLOTS):
        owner = lax.shift_right_logical(anchor[me * SLOTS + slot], 4)
        position = jnp.int32(-1)
        for at, shift in enumerate(SHIFTS):
            hit = owner == wrap(me - shift, INST)
            position = jnp.where(hit, at * MIG + jnp.minimum(counts[at], MIG - 1), position)
            for rank in range(MIG):
                one = at * MIG + rank
                found[one] = jnp.where(hit & (counts[at] == rank), slot, found[one])
            counts[at] = counts[at] + hit.astype(I32)
        positions.append(position)
    return positions, found


def scan_staying(anchor, me):
    rank = jnp.int32(0)
    slots = [jnp.int32(0)] * STAY
    for slot in range(SLOTS):
        hit = lax.shift_right_logical(anchor[me * SLOTS + slot], 4) == me
        for one in range(max(0, slot - MOVES), min(slot + 1, STAY)):
            slots[one] = jnp.where(hit & (rank == one), slot, slots[one])
        rank = rank + hit.astype(I32)
    return slots


def chain_kernel(
    anchor_in, lengths_in, q_in, new_in, hidden_in, kv, weight,
    kv_a, kv_b, early_in, late_in, out, moved_len,
    anchor, lengths, q_rows, new_rows, hidden, q_slots, table, w_blocks,
    asks, asks_in, early, late, back, back_in, tile, tile_in, rows_m,
    send_l, recv_l, send_m, recv_m, delta_l, part_l, delta_m, part_m, rows, acc_m,
    load_sems, w_sems, ask_sems, early_sems, back_sems, tile_sems, late_sems,
    l_sems, m_sems, pl_sems, pm_sems, ready,
):
    inst, section, tp = (lax.axis_index(name) for name in ("inst", "section", "tp"))
    far_half = lax.rem(tp, 2)

    def on_inst(shift):
        return {"inst": wrap(inst + shift, INST)}

    def on_tp(distance):
        return {"tp": wrap(tp + distance, TP)}

    def remote(source, target, sems, at, device):
        return pltpu.make_async_remote_copy(
            src_ref=source, dst_ref=target, send_sem=sems.at[0, at], recv_sem=sems.at[1, at],
            device_id=device, device_id_type=MESH,
        )

    def signal(sem, device):
        pl.semaphore_signal(sem, inc=1, device_id=device, device_id_type=MESH)

    barrier = pltpu.get_barrier_semaphore()
    for shift in SHIFTS:
        signal(barrier, on_inst(shift))
    for distance in (2, 4, 6):
        signal(barrier, on_tp(distance))
    for distance in range(1, SECTIONS):
        pl.when(section + distance < SECTIONS)(
            lambda distance=distance: signal(barrier, {"section": section + distance})
        )

    @pl.when(far_half == 0)
    def _():
        for distance in (1, 3, 5, 7):
            signal(barrier, on_tp(distance))

    small = [
        pltpu.make_async_copy(source, target, load_sems.at[at])
        for at, (source, target) in enumerate(
            (
                (anchor_in, anchor),
                (q_in, q_rows),
                (new_in, new_rows),
                (lengths_in, lengths),
                (hidden_in, hidden),
                (kv.at[0, :, 0, pl.ds(0, CUT)], kv_a),
                (kv.at[0, :, 0, pl.ds(CUT, CTX - CUT)], kv_b),
            )
        )
    ]
    for copy in small:
        copy.start()
    loads = {}
    for distance in ORDER + (0,):
        columns = pl.ds(pl.multiple_of(wrap(tp + distance, TP) * COLS, COLS), COLS)
        loads[distance] = pltpu.make_async_copy(
            weight.at[0, :, columns], w_blocks.at[distance], w_sems.at[distance]
        )
        loads[distance].start()

    small[1].wait()
    small[2].wait()
    queries = q_rows[0].astype(F32)
    pairs = new_rows[0].astype(F32)
    for head in range(GROUP):
        q_slots[:, head, :] = queries[:, head * HD : (head + 1) * HD]
    q_slots[:, 4, :] = pairs[:, :HD]
    q_slots[:, 5, :] = pairs[:, HD:]
    q_slots[:, 6, :] = jnp.zeros((SLOTS, HD), F32)
    q_slots[:, 7, :] = jnp.zeros((SLOTS, HD), F32)
    small[0].wait()
    positions, found = scan_arriving(anchor, inst)
    for at in range(len(SHIFTS)):
        asks[at] = jnp.concatenate([q_slots[found[at * MIG + rank]] for rank in range(MIG)], axis=0).astype(BF)
    leaving = [scan_leaving(anchor, inst, shift) for shift in SHIFTS]
    pl.semaphore_wait(barrier, len(SHIFTS) + 3 + section + 4 * far_half)
    ask_copies = [
        remote(asks.at[at], asks_in.at[at], ask_sems, at, on_inst(-shift)) for at, shift in enumerate(SHIFTS)
    ]
    for copy in ask_copies:
        copy.start()

    @pl.when(far_half == 1)
    def _():
        for distance in (1, 3, 5, 7):
            signal(ready.at[0], on_tp(distance))

    for distance in range(1, SECTIONS):
        pl.when(section >= distance)(
            lambda distance=distance: signal(ready.at[1], {"section": section - distance})
        )

    small[5].wait()
    early_copies, late_copies, back_copies, tile_copies = [], [], [], []
    for at, shift in enumerate(SHIFTS):
        early_copies.append(remote(early.at[at], early_in.at[at], early_sems, at, on_inst(shift)))
        late_copies.append(remote(late.at[at], late_in.at[at], late_sems, at, on_inst(shift)))
        back_copies.append(remote(back.at[at], back_in.at[at], back_sems, at, on_inst(shift)))
        tile_copies.append(remote(tile.at[at], tile_in.at[at], tile_sems, at, on_inst(shift)))
    for at in (1, 0, 2):
        for rank in range(MIG):
            early[at, rank] = kv_a[leaving[at][rank], :EARLY, :]
        early_copies[at].start()
    small[3].wait()
    small[6].wait()
    for at in range(len(SHIFTS)):
        for rank in range(MIG):
            slot = leaving[at][rank]
            late[at, rank, : CUT - EARLY, :] = kv_a[slot, EARLY:, :]
            late[at, rank, CUT - EARLY :, :] = kv_b[slot]

    def attend_at(queries, slots):
        return attend(
            queries,
            [[kv_a[slot, :, :HD], kv_b[slot, :, :HD]] for slot in slots],
            [[kv_a[slot, :, HD:], kv_b[slot, :, HD:]] for slot in slots],
            [lengths[slot] for slot in slots],
        )

    staying = scan_staying(anchor, inst)
    sources = [anchor[inst * SLOTS + slot] & (SLOTS - 1) for slot in staying]
    for one, result in enumerate(attend_at([q_slots[slot] for slot in staying], sources)):
        table[one] = result
    lane = lax.broadcasted_iota(I32, (8, 128), 1)
    for at in range(len(SHIFTS)):
        filled = jnp.zeros((8, 128), I32)
        for rank in range(MIG):
            filled = jnp.where(lane == rank, lengths[leaving[at][rank]], filled)
        tile[at] = filled

    asked = []
    for at in range(len(SHIFTS)):
        ask_copies[at].wait_recv()
        both = asks_in[at].astype(F32)
        asked += [both[rank * 8 : rank * 8 + 8, :] for rank in range(MIG)]
    results = attend_at(asked, [slot for pair in leaving for slot in pair])
    for at in range(len(SHIFTS)):
        back[at] = jnp.concatenate(results[at * MIG : at * MIG + MIG], axis=0).astype(BF)
        back_copies[at].start()
    for copy in tile_copies:
        copy.start()
    for at in (1, 0, 2):
        late_copies[at].start()

    for one in range(STAY, SLOTS):
        table[one] = jnp.zeros((8, HD), F32)
    stay = jnp.concatenate([table[:, head, :] for head in range(GROUP)], axis=1).astype(BF)

    @pl.when(far_half == 0)
    def _():
        pl.semaphore_wait(ready.at[0], 4)

    stay_copies = {}
    own_l = None
    for distance in ORDER + (0,):
        loads[distance].wait()
        share = jnp.dot(stay, w_blocks[distance], preferred_element_type=F32)
        if distance == 0:
            own_l = share
        else:
            send_l[distance] = share.astype(BF)
            copy = remote(send_l.at[distance], recv_l.at[distance], l_sems, distance, on_tp(distance))
            copy.start()
            stay_copies[distance] = copy

    for copy in back_copies:
        copy.wait_recv()
    for at in range(len(SHIFTS)):
        both = back_in[at].astype(F32)
        for rank in range(MIG):
            rows_m[at * MIG + rank] = both[rank * 8 : rank * 8 + 8, :]
    rows_m[6] = jnp.zeros((8, HD), F32)
    rows_m[7] = jnp.zeros((8, HD), F32)
    come = jnp.concatenate([rows_m[:, head, :] for head in range(GROUP)], axis=1).astype(BF)
    half = COLS // 2
    come_copies = {}
    own_m = None
    for distance in ORDER + (0,):
        share = jnp.dot(come, w_blocks[distance], preferred_element_type=F32)
        share = jnp.concatenate([share[:, :half], share[:, half:]], axis=0)
        if distance == 0:
            own_m = share
        else:
            send_m[distance] = share.astype(BF)
            copy = remote(send_m.at[distance], recv_m.at[distance], m_sems, distance, on_tp(distance))
            copy.start()
            come_copies[distance] = copy

    def later(source, target, sems, do):
        for distance in range(1, SECTIONS):

            @pl.when(section + distance < SECTIONS)
            def _(distance=distance):
                do(remote(source, target.at[distance], sems, distance, {"section": section + distance}))

    def start(copy):
        copy.start()

    def sent(copy):
        copy.wait_send()

    pl.when(section < SECTIONS - 1)(lambda: pl.semaphore_wait(ready.at[1], SECTIONS - 1 - section))
    total = own_l
    for distance in ORDER:
        stay_copies[distance].wait_recv()
        total = total + recv_l[distance].astype(F32)
    delta_l[...] = total.astype(BF)
    later(delta_l, part_l, pl_sems, start)
    rows[...] = total
    total = own_m
    for distance in ORDER:
        come_copies[distance].wait_recv()
        total = total + recv_m[distance].astype(F32)
    delta_m[...] = total.astype(BF)
    later(delta_m, part_m, pm_sems, start)
    acc_m[...] = total

    for copy in tile_copies:
        copy.wait_recv()
    lens = jnp.zeros((8, 128), I32)
    for slot in range(SLOTS):
        lens = jnp.where(lane == slot, lengths[anchor[inst * SLOTS + slot] & (SLOTS - 1)], lens)
    for at in range(len(SHIFTS)):
        for rank in range(MIG):
            value = jnp.sum(jnp.where(lane == rank, tile_in[at], 0), axis=1, keepdims=True)
            lens = jnp.where(lane == found[at * MIG + rank], value, lens)
    moved_len[...] = lens

    for distance in range(1, SECTIONS):

        @pl.when(section >= distance)
        def _(distance=distance):
            remote(delta_l, part_l.at[distance], pl_sems, distance, {"section": section}).wait_recv()
            rows[...] += part_l[distance].astype(F32)

    small[4].wait()
    for distance in range(1, SECTIONS):

        @pl.when(section >= distance)
        def _(distance=distance):
            remote(delta_m, part_m.at[distance], pm_sems, distance, {"section": section}).wait_recv()
            acc_m[...] += part_m[distance].astype(F32)

    low, high = acc_m.at[pl.ds(0, 8)], acc_m.at[pl.ds(8, 8)]
    rank = jnp.int32(0)
    lines = []
    for slot in range(SLOTS):
        position = positions[slot]
        place = pl.ds(jnp.maximum(position, 0), 1)
        moved_row = jnp.concatenate([low[place, :], high[place, :]], axis=1)
        stay_row = rows[pl.ds(jnp.minimum(rank, STAY - 1), 1), :]
        lines.append(jnp.where(position >= 0, moved_row, stay_row))
        rank = rank + (position < 0).astype(I32)
    out[...] = (hidden[...].astype(F32) + jnp.concatenate(lines, axis=0)).astype(BF)

    later(delta_l, part_l, pl_sems, sent)
    later(delta_m, part_m, pm_sems, sent)
    for copy in list(stay_copies.values()) + list(come_copies.values()) + back_copies + tile_copies + ask_copies:
        copy.wait_send()
    for copy in early_copies + late_copies:
        copy.wait()


def place_kernel(
    anchor_in, kv_a, kv_b, early_in, late_in, out_rows, lens, out, moved, moved_len, anchor, scalars, sems, more
):
    me = lax.axis_index("inst")
    first = [
        pltpu.make_async_copy(anchor_in, anchor, more.at[0]),
        pltpu.make_async_copy(lens, scalars, more.at[1]),
        pltpu.make_async_copy(out_rows, out.at[0], more.at[2]),
    ]
    for copy in first:
        copy.start()
    first[0].wait()
    positions, _ = scan_arriving(anchor, me)

    def each(do):
        for slot in range(SLOTS):
            source = anchor[me * SLOTS + slot] & (SLOTS - 1)
            position = positions[slot]

            def move(low, high, cut, slot=slot):
                target = moved.at[0, slot, 0]
                do(pltpu.make_async_copy(low, target.at[pl.ds(0, cut)], sems.at[0, slot]))
                do(pltpu.make_async_copy(high, target.at[pl.ds(cut, CTX - cut)], sems.at[1, slot]))

            @pl.when(position < 0)
            def _(source=source, move=move):
                move(kv_a.at[source], kv_b.at[source], CUT)

            @pl.when(position >= 0)
            def _(position=position, move=move):
                at, rank = lax.shift_right_logical(position, 1), position & 1
                move(early_in.at[at, rank], late_in.at[at, rank], EARLY)

    each(lambda copy: copy.start())
    first[1].wait()
    for slot in range(SLOTS):
        moved_len[slot] = scalars[0, slot]
    first[2].wait()
    each(lambda copy: copy.wait())


def specs(*spaces):
    return [pl.BlockSpec(memory_space=space) for space in spaces]


def body(hidden, queries, new_kv, kv_cache, lengths, anchor, out_weight):
    vmem, smem, hbm = pltpu.VMEM, pltpu.SMEM, pltpu.HBM
    dma = pltpu.SemaphoreType.DMA
    hidden, queries, new_kv, kv_cache, lengths, anchor, out_weight = (
        pltpu.with_memory_space_constraint(value, hbm)
        for value in (hidden, queries, new_kv, kv_cache, lengths, anchor, out_weight)
    )
    shapes = [
        ((SLOTS, CUT, 2 * HD), BF), ((SLOTS, CTX - CUT, 2 * HD), BF),
        ((3, MIG, EARLY, 2 * HD), BF), ((3, MIG, LATE, 2 * HD), BF),
        ((SLOTS, COLS), BF), ((8, 128), I32),
    ]
    half = COLS // 2
    made = pl.pallas_call(
        chain_kernel,
        out_shape=[vmem(*shape) for shape in shapes],
        in_specs=specs(*[hbm] * 7),
        out_specs=specs(*[vmem] * 6),
        scratch_shapes=[
            smem((INST * SLOTS,), I32), smem((SLOTS,), I32),
            vmem(queries.shape, BF), vmem(new_kv.shape, BF), vmem((SLOTS, COLS), BF),
            vmem((SLOTS, 8, HD), F32), vmem((SLOTS, 8, HD), F32),
            vmem((TP, GROUP * HD, COLS), BF),
            vmem((3, 16, HD), BF), vmem((3, 16, HD), BF),
            vmem((3, MIG, EARLY, 2 * HD), BF), vmem((3, MIG, LATE, 2 * HD), BF),
            vmem((3, 16, HD), BF), vmem((3, 16, HD), BF),
            vmem((3, 8, 128), I32), vmem((3, 8, 128), I32),
            vmem((8, 8, HD), F32),
            vmem((TP, 16, COLS), BF), vmem((TP, 16, COLS), BF),
            vmem((TP, 16, half), BF), vmem((TP, 16, half), BF),
            vmem((16, COLS), BF), vmem((SECTIONS, 16, COLS), BF),
            vmem((16, half), BF), vmem((SECTIONS, 16, half), BF),
            vmem((SLOTS, COLS), F32), vmem((16, half), F32),
            dma((7,)), dma((TP,)), dma((2, 3)), dma((2, 3)), dma((2, 3)), dma((2, 3)), dma((2, 3)),
            dma((2, TP)), dma((2, TP)), dma((2, SECTIONS)), dma((2, SECTIONS)),
            pltpu.SemaphoreType.REGULAR((2,)),
        ],
        compiler_params=pltpu.CompilerParams(
            collective_id=0, has_side_effects=True, vmem_limit_bytes=32 << 20
        ),
        name="chain",
    )(anchor, lengths, queries, new_kv, hidden, kv_cache, out_weight)
    out, moved, moved_len = pl.pallas_call(
        place_kernel,
        out_shape=[
            jax.ShapeDtypeStruct((1, SLOTS, COLS), BF),
            jax.ShapeDtypeStruct(kv_cache.shape, BF),
            jax.ShapeDtypeStruct((SLOTS,), I32),
        ],
        in_specs=specs(hbm, *[vmem] * 6),
        out_specs=specs(hbm, hbm, smem),
        scratch_shapes=[smem((INST * SLOTS,), I32), smem((8, 128), I32), dma((2, SLOTS)), dma((3,))],
        compiler_params=pltpu.CompilerParams(vmem_limit_bytes=8 << 20),
        name="place",
    )(anchor, *made)
    return out, moved, moved_len


def solution(mesh):
    return jax.shard_map(
        body,
        mesh=mesh,
        in_specs=(
            P("inst", "tp"),
            P("section", "inst", "tp"),
            P("section", "inst", "tp"),
            P("section", "inst", "tp", None, None),
            P("inst"),
            P(),
            P("section", "tp", None),
        ),
        out_specs=(P("section", "inst", "tp"), P("section", "inst", "tp", None, None), P("inst")),
        check_vma=False,
    )
```

```python
import functools
import math

import jax
import jax.numpy as jnp
from jax import lax
from jax.experimental import pallas as pl
from jax.experimental.pallas import tpu as pltpu
from jax.sharding import PartitionSpec as P

MESH = pl.DeviceIdType.MESH
BF = jnp.bfloat16
F32 = jnp.float32
I32 = jnp.int32

INST = 4
TP = 8
SECTIONS = 8
SLOTS = 16
MIG = 2
GROUP = 4
HD = 128
CTX = 512
MODEL = 8192
COLS = MODEL // TP
FOLD_L = (SLOTS - 6) * COLS // 16
FOLD_M = 6 * COLS // 16
CUT = 128
EARLY = 96
LATE = CTX - EARLY
SHIFTS = (1, 2, 3)
MOVES = len(SHIFTS) * MIG
STAY = SLOTS - MOVES
ORDER = (3, 5, 1, 7, 4, 2, 6)
INV_ROOT = 1.0 / math.sqrt(HD)

def wrap(value, count):
    return lax.rem(value + count, count)


def fold_stay(rows):
    step = COLS // 4
    tail = jnp.concatenate([rows[8:10, k * step : (k + 1) * step] for k in range(4)], axis=0)
    wide = jnp.concatenate([rows[:8], tail], axis=1)
    return jnp.concatenate([wide[:, :FOLD_L], wide[:, FOLD_L:]], axis=0)


def unfold_stay(folded):
    wide = jnp.concatenate([folded[:8], folded[8:]], axis=1)
    tail = jnp.concatenate([wide[2 * k : 2 * k + 2, COLS:] for k in range(4)], axis=1)
    return wide[:, :COLS], tail


def fold_come(rows):
    step = COLS // 4
    rest = [rows[k : k + 1, 3 * step :] for k in range(6)]
    wide = jnp.concatenate(
        [rows[:6, : 3 * step], jnp.concatenate(rest[:3], axis=1), jnp.concatenate(rest[3:], axis=1)], axis=0
    )
    return jnp.concatenate([wide[:, :FOLD_M], wide[:, FOLD_M:]], axis=0)


def unfold_come(folded):
    step = COLS // 4
    wide = jnp.concatenate([folded[:8], folded[8:]], axis=1)
    rest = [wide[6 + k // 3 : 7 + k // 3, (k % 3) * step : (k % 3 + 1) * step] for k in range(6)]
    return jnp.concatenate([wide[:6], jnp.concatenate(rest, axis=0)], axis=1)


def attend(queries, keys, values, lengths):
    scores = []
    for query, blocks in zip(queries, keys):
        rows = query.astype(BF)
        parts = [
            lax.dot_general(rows, block, (((1,), (1,)), ((), ())), preferred_element_type=F32) for block in blocks
        ]
        scores.append(jnp.concatenate(parts, axis=1))
    place = lax.broadcasted_iota(I32, (8, CTX), 1)
    probs = []
    for query, score, length in zip(queries, scores, lengths):
        score = jnp.where(place < length, score * INV_ROOT, -jnp.inf)
        new_score = jnp.sum(query * query[4:5, :], axis=1, keepdims=True) * INV_ROOT
        top = jnp.maximum(jnp.max(score, axis=1, keepdims=True), new_score)
        expo = jnp.exp(score - top)
        new_expo = jnp.exp(new_score - top)
        scale = 1.0 / (jnp.sum(expo, axis=1, keepdims=True) + new_expo)
        probs.append(((expo * scale).astype(BF), (new_expo * scale).astype(BF).astype(F32)))
    results = []
    for query, (prob, new_prob), blocks in zip(queries, probs, values):
        result = new_prob * query[5:6, :]
        start = 0
        for block in blocks:
            stop = start + block.shape[0]
            result = result + jnp.dot(prob[:, start:stop], block, preferred_element_type=F32)
            start = stop
        results.append(result)
    return results


def scan_leaving(anchor, me, shift):
    dest = wrap(me + shift, INST)
    count = jnp.int32(0)
    picked = [jnp.int32(0)] * MIG
    for slot in range(SLOTS):
        source = anchor[dest * SLOTS + slot]
        hit = lax.shift_right_logical(source, 4) == me
        for rank in range(MIG):
            picked[rank] = jnp.where(hit & (count == rank), source & (SLOTS - 1), picked[rank])
        count = count + hit.astype(I32)
    return picked


def scan_arriving(anchor, me):
    counts = [jnp.int32(0)] * len(SHIFTS)
    found = [jnp.int32(0)] * MOVES
    positions = []
    for slot in range(SLOTS):
        owner = lax.shift_right_logical(anchor[me * SLOTS + slot], 4)
        position = jnp.int32(-1)
        for at, shift in enumerate(SHIFTS):
            hit = owner == wrap(me - shift, INST)
            position = jnp.where(hit, at * MIG + jnp.minimum(counts[at], MIG - 1), position)
            for rank in range(MIG):
                one = at * MIG + rank
                found[one] = jnp.where(hit & (counts[at] == rank), slot, found[one])
            counts[at] = counts[at] + hit.astype(I32)
        positions.append(position)
    return positions, found


def scan_staying(anchor, me):
    rank = jnp.int32(0)
    slots = [jnp.int32(0)] * STAY
    for slot in range(SLOTS):
        hit = lax.shift_right_logical(anchor[me * SLOTS + slot], 4) == me
        for one in range(max(0, slot - MOVES), min(slot + 1, STAY)):
            slots[one] = jnp.where(hit & (rank == one), slot, slots[one])
        rank = rank + hit.astype(I32)
    return slots


def chain_kernel(
    anchor_in, lengths_in, q_in, new_in, hidden_in, kv, weight,
    kv_a, kv_b, early_in, late_in, out, notes,
    anchor, lengths, q_rows, new_rows, hidden, q_slots, table, w_blocks,
    asks, asks_in, early, late, back, back_in, tile, tile_in, rows_m,
    send_l, recv_l, send_m, recv_m, delta_l, part_l, delta_m, part_m, rows, acc_m, lines_l, lines_m,
    load_sems, w_sems, ask_sems, early_sems, back_sems, tile_sems, late_sems,
    l_sems, m_sems, pl_sems, pm_sems, ready,
):
    inst, section, tp = (lax.axis_index(name) for name in ("inst", "section", "tp"))
    far_half = lax.rem(tp, 2)

    def on_inst(shift):
        return {"inst": wrap(inst + shift, INST)}

    def on_tp(distance):
        return {"tp": wrap(tp + distance, TP)}

    def remote(source, target, sems, at, device):
        return pltpu.make_async_remote_copy(
            src_ref=source, dst_ref=target, send_sem=sems.at[0, at], recv_sem=sems.at[1, at],
            device_id=device, device_id_type=MESH,
        )

    def signal(sem, device):
        pl.semaphore_signal(sem, inc=1, device_id=device, device_id_type=MESH)

    barrier = pltpu.get_barrier_semaphore()
    for shift in SHIFTS:
        signal(barrier, on_inst(shift))
    for distance in (2, 4, 6):
        signal(barrier, on_tp(distance))
    for distance in range(1, SECTIONS):
        pl.when(section + distance < SECTIONS)(
            lambda distance=distance: signal(barrier, {"section": section + distance})
        )

    @pl.when(far_half == 0)
    def _():
        for distance in (1, 3, 5, 7):
            signal(barrier, on_tp(distance))

    small = [
        pltpu.make_async_copy(source, target, load_sems.at[at])
        for at, (source, target) in enumerate(
            (
                (anchor_in, anchor),
                (q_in, q_rows),
                (new_in, new_rows),
                (lengths_in, lengths),
                (hidden_in, hidden),
                (kv.at[0, :, 0, pl.ds(0, CUT)], kv_a),
                (kv.at[0, :, 0, pl.ds(CUT, CTX - CUT)], kv_b),
            )
        )
    ]
    for copy in small:
        copy.start()
    small[1].wait()
    small[2].wait()
    queries = q_rows[0].astype(F32)
    pairs = new_rows[0].astype(F32)
    for head in range(GROUP):
        q_slots[:, head, :] = queries[:, head * HD : (head + 1) * HD]
    q_slots[:, 4, :] = pairs[:, :HD]
    q_slots[:, 5, :] = pairs[:, HD:]
    q_slots[:, 6, :] = jnp.zeros((SLOTS, HD), F32)
    q_slots[:, 7, :] = jnp.zeros((SLOTS, HD), F32)
    small[0].wait()
    positions, found = scan_arriving(anchor, inst)
    for at in range(len(SHIFTS)):
        asks[at] = jnp.concatenate([q_slots[found[at * MIG + rank]] for rank in range(MIG)], axis=0).astype(BF)
    leaving = [scan_leaving(anchor, inst, shift) for shift in SHIFTS]
    pl.semaphore_wait(barrier, len(SHIFTS) + 3 + section + 4 * far_half)
    ask_copies = [
        remote(asks.at[at], asks_in.at[at], ask_sems, at, on_inst(-shift)) for at, shift in enumerate(SHIFTS)
    ]
    for copy in ask_copies:
        copy.start()

    @pl.when(far_half == 1)
    def _():
        for distance in (1, 3, 5, 7):
            signal(ready.at[0], on_tp(distance))

    for distance in range(1, SECTIONS):
        pl.when(section >= distance)(
            lambda distance=distance: signal(ready.at[1], {"section": section - distance})
        )

    small[5].wait()
    early_copies, late_copies, back_copies, tile_copies = [], [], [], []
    for at, shift in enumerate(SHIFTS):
        early_copies.append(remote(early.at[at], early_in.at[at], early_sems, at, on_inst(shift)))
        late_copies.append(remote(late.at[at], late_in.at[at], late_sems, at, on_inst(shift)))
        back_copies.append(remote(back.at[at], back_in.at[at], back_sems, at, on_inst(shift)))
        tile_copies.append(remote(tile.at[at], tile_in.at[at], tile_sems, at, on_inst(shift)))
    for at in (1, 0, 2):
        for rank in range(MIG):
            early[at, rank] = kv_a[leaving[at][rank], :EARLY, :]
        early_copies[at].start()
    small[3].wait()
    small[6].wait()
    loads = {}
    for distance in ORDER + (0,):
        columns = pl.ds(pl.multiple_of(wrap(tp + distance, TP) * COLS, COLS), COLS)
        loads[distance] = pltpu.make_async_copy(
            weight.at[0, :, columns], w_blocks.at[distance], w_sems.at[distance]
        )
        loads[distance].start()
    for at in range(len(SHIFTS)):
        for rank in range(MIG):
            slot = leaving[at][rank]
            late[at, rank, : CUT - EARLY, :] = kv_a[slot, EARLY:, :]
            late[at, rank, CUT - EARLY :, :] = kv_b[slot]

    def attend_at(queries, slots):
        return attend(
            queries,
            [[kv_a[slot, :, :HD], kv_b[slot, :, :HD]] for slot in slots],
            [[kv_a[slot, :, HD:], kv_b[slot, :, HD:]] for slot in slots],
            [lengths[slot] for slot in slots],
        )

    staying = scan_staying(anchor, inst)
    sources = [anchor[inst * SLOTS + slot] & (SLOTS - 1) for slot in staying]
    for one, result in enumerate(attend_at([q_slots[slot] for slot in staying], sources)):
        table[one] = result
    lane = lax.broadcasted_iota(I32, (8, 128), 1)
    for at in range(len(SHIFTS)):
        filled = jnp.zeros((8, 128), I32)
        for rank in range(MIG):
            filled = jnp.where(lane == rank, lengths[leaving[at][rank]], filled)
        tile[at] = filled

    asked = []
    for at in range(len(SHIFTS)):
        ask_copies[at].wait_recv()
        both = asks_in[at].astype(F32)
        asked += [both[rank * 8 : rank * 8 + 8, :] for rank in range(MIG)]
    results = attend_at(asked, [slot for pair in leaving for slot in pair])
    for at in range(len(SHIFTS)):
        back[at] = jnp.concatenate(results[at * MIG : at * MIG + MIG], axis=0).astype(BF)
        back_copies[at].start()
    for copy in tile_copies:
        copy.start()
    for at in (1, 0, 2):
        late_copies[at].start()

    for one in range(STAY, SLOTS):
        table[one] = jnp.zeros((8, HD), F32)
    stay = jnp.concatenate([table[:, head, :] for head in range(GROUP)], axis=1).astype(BF)

    @pl.when(far_half == 0)
    def _():
        pl.semaphore_wait(ready.at[0], 4)

    stay_copies = {}
    own_l = None
    for distance in ORDER + (0,):
        loads[distance].wait()
        share = fold_stay(jnp.dot(stay, w_blocks[distance], preferred_element_type=F32))
        if distance == 0:
            own_l = share
        else:
            send_l[distance] = share.astype(BF)
            copy = remote(send_l.at[distance], recv_l.at[distance], l_sems, distance, on_tp(distance))
            copy.start()
            stay_copies[distance] = copy

    for copy in back_copies:
        copy.wait_recv()
    for at in range(len(SHIFTS)):
        both = back_in[at].astype(F32)
        for rank in range(MIG):
            rows_m[at * MIG + rank] = both[rank * 8 : rank * 8 + 8, :]
    rows_m[6] = jnp.zeros((8, HD), F32)
    rows_m[7] = jnp.zeros((8, HD), F32)
    come = jnp.concatenate([rows_m[:, head, :] for head in range(GROUP)], axis=1).astype(BF)
    come_copies = {}
    own_m = None
    for distance in ORDER + (0,):
        share = fold_come(jnp.dot(come, w_blocks[distance], preferred_element_type=F32))
        if distance == 0:
            own_m = share
        else:
            send_m[distance] = share.astype(BF)
            copy = remote(send_m.at[distance], recv_m.at[distance], m_sems, distance, on_tp(distance))
            copy.start()
            come_copies[distance] = copy

    def later(source, target, sems, do):
        for distance in range(1, SECTIONS):

            @pl.when(section + distance < SECTIONS)
            def _(distance=distance):
                do(remote(source, target.at[distance], sems, distance, {"section": section + distance}))

    def start(copy):
        copy.start()

    def sent(copy):
        copy.wait_send()

    pl.when(section < SECTIONS - 1)(lambda: pl.semaphore_wait(ready.at[1], SECTIONS - 1 - section))
    total = own_l
    for distance in ORDER:
        stay_copies[distance].wait_recv()
        total = total + recv_l[distance].astype(F32)
    delta_l[...] = total.astype(BF)
    later(delta_l, part_l, pl_sems, start)
    rows[...] = total
    total = own_m
    for distance in ORDER:
        come_copies[distance].wait_recv()
        total = total + recv_m[distance].astype(F32)
    delta_m[...] = total.astype(BF)
    later(delta_m, part_m, pm_sems, start)
    acc_m[...] = total

    for copy in tile_copies:
        copy.wait_recv()
    lens = jnp.zeros((8, 128), I32)
    plan = jnp.zeros((8, 128), I32)
    for slot in range(SLOTS):
        source = anchor[inst * SLOTS + slot] & (SLOTS - 1)
        lens = jnp.where(lane == slot, lengths[source], lens)
        plan = jnp.where(lane == slot, jnp.where(positions[slot] < 0, source, SLOTS + positions[slot]), plan)
    for at in range(len(SHIFTS)):
        for rank in range(MIG):
            value = jnp.sum(jnp.where(lane == rank, tile_in[at], 0), axis=1, keepdims=True)
            lens = jnp.where(lane == found[at * MIG + rank], value, lens)
    row = lax.broadcasted_iota(I32, (8, 128), 0)
    notes[...] = jnp.where(row == 0, lens, plan)

    for distance in range(1, SECTIONS):

        @pl.when(section >= distance)
        def _(distance=distance):
            remote(delta_l, part_l.at[distance], pl_sems, distance, {"section": section}).wait_recv()
            rows[...] += part_l[distance].astype(F32)

    small[4].wait()
    for distance in range(1, SECTIONS):

        @pl.when(section >= distance)
        def _(distance=distance):
            remote(delta_m, part_m.at[distance], pm_sems, distance, {"section": section}).wait_recv()
            acc_m[...] += part_m[distance].astype(F32)

    lines_l[0:8], lines_l[8:10] = unfold_stay(rows[...])
    lines_m[0:6] = unfold_come(acc_m[...])
    rank = jnp.int32(0)
    lines = []
    for slot in range(SLOTS):
        position = positions[slot]
        moved_row = lines_m[pl.ds(jnp.maximum(position, 0), 1), :]
        stay_row = lines_l[pl.ds(jnp.minimum(rank, STAY - 1), 1), :]
        lines.append(jnp.where(position >= 0, moved_row, stay_row))
        rank = rank + (position < 0).astype(I32)
    out[...] = (hidden[...].astype(F32) + jnp.concatenate(lines, axis=0)).astype(BF)

    later(delta_l, part_l, pl_sems, sent)
    later(delta_m, part_m, pm_sems, sent)
    for copy in list(stay_copies.values()) + list(come_copies.values()) + back_copies + tile_copies + ask_copies:
        copy.wait_send()
    for copy in early_copies + late_copies:
        copy.wait()


def place_kernel(kv_a, kv_b, early_in, late_in, out_rows, notes, out, moved, moved_len, plan, lens, sems):
    first = [
        pltpu.make_async_copy(notes, plan, sems.at[0]),
        pltpu.make_async_copy(out_rows, out.at[0], sems.at[1]),
    ]
    for copy in first:
        copy.start()
    first[0].wait()
    for slot in range(SLOTS):
        place = plan[1, slot]

        def move(low, high, cut, slot=slot):
            target = moved.at[0, slot, 0]
            pltpu.make_async_copy(low, target.at[pl.ds(0, cut)], sems.at[2]).start()
            pltpu.make_async_copy(high, target.at[pl.ds(cut, CTX - cut)], sems.at[2]).start()

        @pl.when(place < SLOTS)
        def _(place=place, move=move):
            move(kv_a.at[place], kv_b.at[place], CUT)

        @pl.when(place >= SLOTS)
        def _(place=place, move=move):
            at, rank = lax.shift_right_logical(place - SLOTS, 1), place & 1
            move(early_in.at[at, rank], late_in.at[at, rank], EARLY)

    for slot in range(SLOTS):
        lens[slot] = plan[0, slot]
    last = pltpu.make_async_copy(lens, moved_len, sems.at[3])
    last.start()
    first[1].wait()
    pltpu.make_async_copy(moved, moved, sems.at[2]).wait()
    last.wait()


def specs(*spaces):
    return [pl.BlockSpec(memory_space=space) for space in spaces]


def body(hidden, queries, new_kv, kv_cache, lengths, anchor, out_weight):
    vmem, smem, hbm = pltpu.VMEM, pltpu.SMEM, pltpu.HBM
    dma = pltpu.SemaphoreType.DMA
    hidden, queries, new_kv, kv_cache, lengths, anchor, out_weight = (
        pltpu.with_memory_space_constraint(value, hbm)
        for value in (hidden, queries, new_kv, kv_cache, lengths, anchor, out_weight)
    )
    shapes = [
        ((SLOTS, CUT, 2 * HD), BF), ((SLOTS, CTX - CUT, 2 * HD), BF),
        ((3, MIG, EARLY, 2 * HD), BF), ((3, MIG, LATE, 2 * HD), BF),
        ((SLOTS, COLS), BF), ((8, 128), I32),
    ]
    made = pl.pallas_call(
        chain_kernel,
        out_shape=[vmem(*shape) for shape in shapes],
        in_specs=specs(*[hbm] * 7),
        out_specs=specs(*[vmem] * 6),
        scratch_shapes=[
            smem((INST * SLOTS,), I32), smem((SLOTS,), I32),
            vmem(queries.shape, BF), vmem(new_kv.shape, BF), vmem((SLOTS, COLS), BF),
            vmem((SLOTS, 8, HD), F32), vmem((SLOTS, 8, HD), F32),
            vmem((TP, GROUP * HD, COLS), BF),
            vmem((3, 16, HD), BF), vmem((3, 16, HD), BF),
            vmem((3, MIG, EARLY, 2 * HD), BF), vmem((3, MIG, LATE, 2 * HD), BF),
            vmem((3, 16, HD), BF), vmem((3, 16, HD), BF),
            vmem((3, 8, 128), I32), vmem((3, 8, 128), I32),
            vmem((8, 8, HD), F32),
            vmem((TP, 16, FOLD_L), BF), vmem((TP, 16, FOLD_L), BF),
            vmem((TP, 16, FOLD_M), BF), vmem((TP, 16, FOLD_M), BF),
            vmem((16, FOLD_L), BF), vmem((SECTIONS, 16, FOLD_L), BF),
            vmem((16, FOLD_M), BF), vmem((SECTIONS, 16, FOLD_M), BF),
            vmem((16, FOLD_L), F32), vmem((16, FOLD_M), F32),
            vmem((STAY, COLS), F32), vmem((MOVES, COLS), F32),
            dma((7,)), dma((TP,)), dma((2, 3)), dma((2, 3)), dma((2, 3)), dma((2, 3)), dma((2, 3)),
            dma((2, TP)), dma((2, TP)), dma((2, SECTIONS)), dma((2, SECTIONS)),
            pltpu.SemaphoreType.REGULAR((2,)),
        ],
        compiler_params=pltpu.CompilerParams(
            collective_id=0, has_side_effects=True, vmem_limit_bytes=32 << 20
        ),
        name="chain",
    )(anchor, lengths, queries, new_kv, hidden, kv_cache, out_weight)
    out, moved, moved_len = pl.pallas_call(
        place_kernel,
        out_shape=[
            jax.ShapeDtypeStruct((1, SLOTS, COLS), BF),
            jax.ShapeDtypeStruct(kv_cache.shape, BF),
            jax.ShapeDtypeStruct((SLOTS,), I32),
        ],
        in_specs=specs(*[vmem] * 6),
        out_specs=specs(hbm, hbm, hbm),
        scratch_shapes=[smem((8, 128), I32), smem((SLOTS,), I32), dma((4,))],
        compiler_params=pltpu.CompilerParams(vmem_limit_bytes=8 << 20),
        name="place",
    )(*made)
    return out, moved, moved_len


def solution(mesh):
    return jax.shard_map(
        body,
        mesh=mesh,
        in_specs=(
            P("inst", "tp"),
            P("section", "inst", "tp"),
            P("section", "inst", "tp"),
            P("section", "inst", "tp", None, None),
            P("inst"),
            P(),
            P("section", "tp", None),
        ),
        out_specs=(P("section", "inst", "tp"), P("section", "inst", "tp", None, None), P("inst")),
        check_vma=False,
    )
```

```python
import functools
import math

import jax
import jax.numpy as jnp
from jax import lax
from jax.experimental import pallas as pl
from jax.experimental.pallas import tpu as pltpu
from jax.sharding import PartitionSpec as P

MESH = pl.DeviceIdType.MESH
BF = jnp.bfloat16
F32 = jnp.float32
I32 = jnp.int32

INST = 4
TP = 8
SECTIONS = 8
SLOTS = 16
MIG = 2
GROUP = 4
HD = 128
CTX = 512
MODEL = 8192
COLS = MODEL // TP
FOLD_L = (SLOTS - 6) * COLS // 16
FOLD_M = 6 * COLS // 16
EARLY = 128
LATE = CTX - EARLY
SHIFTS = (1, 2, 3)
MOVES = len(SHIFTS) * MIG
STAY = SLOTS - MOVES
ORDER = (3, 5, 1, 7, 4, 2, 6)
INV_ROOT = 1.0 / math.sqrt(HD)

def wrap(value, count):
    return lax.rem(value + count, count)


def fold_stay(rows):
    step = COLS // 4
    tail = jnp.concatenate([rows[8:10, k * step : (k + 1) * step] for k in range(4)], axis=0)
    wide = jnp.concatenate([rows[:8], tail], axis=1)
    return jnp.concatenate([wide[:, :FOLD_L], wide[:, FOLD_L:]], axis=0)


def unfold_stay(folded):
    wide = jnp.concatenate([folded[:8], folded[8:]], axis=1)
    tail = jnp.concatenate([wide[2 * k : 2 * k + 2, COLS:] for k in range(4)], axis=1)
    return wide[:, :COLS], tail


def fold_come(rows):
    step = COLS // 4
    rest = [rows[k : k + 1, 3 * step :] for k in range(6)]
    wide = jnp.concatenate(
        [rows[:6, : 3 * step], jnp.concatenate(rest[:3], axis=1), jnp.concatenate(rest[3:], axis=1)], axis=0
    )
    return jnp.concatenate([wide[:, :FOLD_M], wide[:, FOLD_M:]], axis=0)


def unfold_come(folded):
    step = COLS // 4
    wide = jnp.concatenate([folded[:8], folded[8:]], axis=1)
    rest = [wide[6 + k // 3 : 7 + k // 3, (k % 3) * step : (k % 3 + 1) * step] for k in range(6)]
    return jnp.concatenate([wide[:6], jnp.concatenate(rest, axis=0)], axis=1)


def attend(queries, keys, values, lengths):
    scores = []
    for query, blocks in zip(queries, keys):
        rows = query.astype(BF)
        parts = [
            lax.dot_general(rows, block, (((1,), (1,)), ((), ())), preferred_element_type=F32) for block in blocks
        ]
        scores.append(jnp.concatenate(parts, axis=1))
    place = lax.broadcasted_iota(I32, (8, CTX), 1)
    probs = []
    for query, score, length in zip(queries, scores, lengths):
        score = jnp.where(place < length, score * INV_ROOT, -jnp.inf)
        new_score = jnp.sum(query * query[4:5, :], axis=1, keepdims=True) * INV_ROOT
        top = jnp.maximum(jnp.max(score, axis=1, keepdims=True), new_score)
        expo = jnp.exp(score - top)
        new_expo = jnp.exp(new_score - top)
        scale = 1.0 / (jnp.sum(expo, axis=1, keepdims=True) + new_expo)
        probs.append(((expo * scale).astype(BF), (new_expo * scale).astype(BF).astype(F32)))
    results = []
    for query, (prob, new_prob), blocks in zip(queries, probs, values):
        result = new_prob * query[5:6, :]
        start = 0
        for block in blocks:
            stop = start + block.shape[0]
            result = result + jnp.dot(prob[:, start:stop], block, preferred_element_type=F32)
            start = stop
        results.append(result)
    return results


def scan_leaving(anchor, me, shift):
    dest = wrap(me + shift, INST)
    count = jnp.int32(0)
    picked = [jnp.int32(0)] * MIG
    for slot in range(SLOTS):
        source = anchor[dest * SLOTS + slot]
        hit = lax.shift_right_logical(source, 4) == me
        for rank in range(MIG):
            picked[rank] = jnp.where(hit & (count == rank), source & (SLOTS - 1), picked[rank])
        count = count + hit.astype(I32)
    return picked


def scan_arriving(anchor, me):
    counts = [jnp.int32(0)] * len(SHIFTS)
    found = [jnp.int32(0)] * MOVES
    positions = []
    for slot in range(SLOTS):
        owner = lax.shift_right_logical(anchor[me * SLOTS + slot], 4)
        position = jnp.int32(-1)
        for at, shift in enumerate(SHIFTS):
            hit = owner == wrap(me - shift, INST)
            position = jnp.where(hit, at * MIG + jnp.minimum(counts[at], MIG - 1), position)
            for rank in range(MIG):
                one = at * MIG + rank
                found[one] = jnp.where(hit & (counts[at] == rank), slot, found[one])
            counts[at] = counts[at] + hit.astype(I32)
        positions.append(position)
    return positions, found


def scan_staying(anchor, me):
    rank = jnp.int32(0)
    slots = [jnp.int32(0)] * STAY
    for slot in range(SLOTS):
        hit = lax.shift_right_logical(anchor[me * SLOTS + slot], 4) == me
        for one in range(max(0, slot - MOVES), min(slot + 1, STAY)):
            slots[one] = jnp.where(hit & (rank == one), slot, slots[one])
        rank = rank + hit.astype(I32)
    return slots


def chain_kernel(
    anchor_in, lengths_in, q_in, new_in, hidden_in, kv, weight,
    kv_a, kv_b, early_in, late_in, out, notes,
    anchor, lengths, q_rows, new_rows, hidden, q_slots, table, w_blocks,
    asks, asks_in, early, late, back, back_in, tile, tile_in, rows_m,
    send_l, recv_l, send_m, recv_m, delta_l, part_l, delta_m, part_m, rows, acc_m, lines_l, lines_m,
    load_sems, w_sems, ask_sems, early_sems, back_sems, tile_sems, late_sems,
    l_sems, m_sems, pl_sems, pm_sems, ready,
):
    inst, section, tp = (lax.axis_index(name) for name in ("inst", "section", "tp"))
    far_half, row = lax.rem(tp, 2), lax.div(tp, 2)
    last = far_half * lax.div(row, TP // 2 - 1)

    def on_inst(shift):
        return {"inst": wrap(inst + shift, INST)}

    def on_tp(distance):
        return {"tp": wrap(tp + distance, TP)}

    def remote(source, target, sems, at, device):
        return pltpu.make_async_remote_copy(
            src_ref=source, dst_ref=target, send_sem=sems.at[0, at], recv_sem=sems.at[1, at],
            device_id=device, device_id_type=MESH,
        )

    def signal(sem, device):
        pl.semaphore_signal(sem, inc=1, device_id=device, device_id_type=MESH)

    barrier = pltpu.get_barrier_semaphore()
    for shift in SHIFTS:
        signal(barrier, on_inst(shift))
    small = [
        pltpu.make_async_copy(source, target, load_sems.at[at])
        for at, (source, target) in enumerate(
            (
                (anchor_in, anchor),
                (q_in, q_rows),
                (new_in, new_rows),
                (lengths_in, lengths),
                (hidden_in, hidden),
                (kv.at[0, :, 0, pl.ds(0, EARLY)], kv_a),
                (kv.at[0, :, 0, pl.ds(EARLY, CTX - EARLY)], kv_b),
            )
        )
    ]
    for copy in small:
        copy.start()
    for step in (1, 2, 3):
        pl.when(row + step < TP // 2)(lambda step=step: signal(barrier, {"tp": tp + 2 * step}))
    for step in range(1, SECTIONS):
        pl.when(section + step < SECTIONS)(lambda step=step: signal(barrier, {"section": section + step}))

    pl.when(far_half == 0)(lambda: signal(barrier, {"tp": TP - 1}))

    small[1].wait()
    small[2].wait()
    queries = q_rows[0].astype(F32)
    pairs = new_rows[0].astype(F32)
    for head in range(GROUP):
        q_slots[:, head, :] = queries[:, head * HD : (head + 1) * HD]
    q_slots[:, 4, :] = pairs[:, :HD]
    q_slots[:, 5, :] = pairs[:, HD:]
    q_slots[:, 6, :] = jnp.zeros((SLOTS, HD), F32)
    q_slots[:, 7, :] = jnp.zeros((SLOTS, HD), F32)
    small[0].wait()
    positions, found = scan_arriving(anchor, inst)
    for at in range(len(SHIFTS)):
        asks[at] = jnp.concatenate([q_slots[found[at * MIG + rank]] for rank in range(MIG)], axis=0).astype(BF)
    leaving = [scan_leaving(anchor, inst, shift) for shift in SHIFTS]

    small[5].wait()
    early_copies, late_copies, back_copies, tile_copies = [], [], [], []
    for at, shift in enumerate(SHIFTS):
        early_copies.append(remote(early.at[at], early_in.at[at], early_sems, at, on_inst(shift)))
        late_copies.append(remote(late.at[at], late_in.at[at], late_sems, at, on_inst(shift)))
        back_copies.append(remote(back.at[at], back_in.at[at], back_sems, at, on_inst(shift)))
        tile_copies.append(remote(tile.at[at], tile_in.at[at], tile_sems, at, on_inst(shift)))
    for at in range(len(SHIFTS)):
        for rank in range(MIG):
            early[at, rank] = kv_a[leaving[at][rank]]
    pl.semaphore_wait(barrier, len(SHIFTS) + row + section + last * (TP // 2))
    ask_copies = [
        remote(asks.at[at], asks_in.at[at], ask_sems, at, on_inst(-shift)) for at, shift in enumerate(SHIFTS)
    ]
    for copy in ask_copies:
        copy.start()

    for at in (1, 0, 2):
        early_copies[at].start()

    @pl.when(last == 1)
    def _():
        for step in range(TP // 2):
            signal(ready.at[0], {"tp": 2 * step})

    for step in (1, 2, 3):
        pl.when(row >= step)(lambda step=step: signal(ready.at[0], {"tp": tp - 2 * step}))
    for step in range(1, SECTIONS):
        pl.when(section >= step)(lambda step=step: signal(ready.at[1], {"section": section - step}))

    small[3].wait()
    small[6].wait()
    loads = {}
    for distance in ORDER + (0,):
        columns = pl.ds(pl.multiple_of(wrap(tp + distance, TP) * COLS, COLS), COLS)
        loads[distance] = pltpu.make_async_copy(
            weight.at[0, :, columns], w_blocks.at[distance], w_sems.at[distance]
        )
        loads[distance].start()
    for at in range(len(SHIFTS)):
        for rank in range(MIG):
            slot = leaving[at][rank]
            late[at, rank] = kv_b[slot]

    def attend_at(queries, slots):
        return attend(
            queries,
            [[kv_a[slot, :, :HD], kv_b[slot, :, :HD]] for slot in slots],
            [[kv_a[slot, :, HD:], kv_b[slot, :, HD:]] for slot in slots],
            [lengths[slot] for slot in slots],
        )

    staying = scan_staying(anchor, inst)
    sources = [anchor[inst * SLOTS + slot] & (SLOTS - 1) for slot in staying]
    for one, result in enumerate(attend_at([q_slots[slot] for slot in staying], sources)):
        table[one] = result
    lane = lax.broadcasted_iota(I32, (8, 128), 1)
    for at in range(len(SHIFTS)):
        filled = jnp.zeros((8, 128), I32)
        for rank in range(MIG):
            filled = jnp.where(lane == rank, lengths[leaving[at][rank]], filled)
        tile[at] = filled

    asked = []
    for at in range(len(SHIFTS)):
        ask_copies[at].wait_recv()
        both = asks_in[at].astype(F32)
        asked += [both[rank * 8 : rank * 8 + 8, :] for rank in range(MIG)]
    results = attend_at(asked, [slot for pair in leaving for slot in pair])
    for at in range(len(SHIFTS)):
        back[at] = jnp.concatenate(results[at * MIG : at * MIG + MIG], axis=0).astype(BF)
        back_copies[at].start()
    for copy in tile_copies:
        copy.start()
    for at in (1, 0, 2):
        late_copies[at].start()

    for one in range(STAY, SLOTS):
        table[one] = jnp.zeros((8, HD), F32)
    stay = jnp.concatenate([table[:, head, :] for head in range(GROUP)], axis=1).astype(BF)

    unheard = TP // 2 - 1 - row + 1 - far_half
    pl.when(unheard > 0)(lambda: pl.semaphore_wait(ready.at[0], unheard))

    stay_copies = {}
    own_l = None
    for distance in ORDER + (0,):
        loads[distance].wait()
        share = fold_stay(jnp.dot(stay, w_blocks[distance], preferred_element_type=F32))
        if distance == 0:
            own_l = share
        else:
            send_l[distance] = share.astype(BF)
            copy = remote(send_l.at[distance], recv_l.at[distance], l_sems, distance, on_tp(distance))
            copy.start()
            stay_copies[distance] = copy

    for copy in back_copies:
        copy.wait_recv()
    for at in range(len(SHIFTS)):
        both = back_in[at].astype(F32)
        for rank in range(MIG):
            rows_m[at * MIG + rank] = both[rank * 8 : rank * 8 + 8, :]
    rows_m[6] = jnp.zeros((8, HD), F32)
    rows_m[7] = jnp.zeros((8, HD), F32)
    come = jnp.concatenate([rows_m[:, head, :] for head in range(GROUP)], axis=1).astype(BF)
    come_copies = {}
    own_m = None
    for distance in ORDER + (0,):
        share = fold_come(jnp.dot(come, w_blocks[distance], preferred_element_type=F32))
        if distance == 0:
            own_m = share
        else:
            send_m[distance] = share.astype(BF)
            copy = remote(send_m.at[distance], recv_m.at[distance], m_sems, distance, on_tp(distance))
            copy.start()
            come_copies[distance] = copy

    def later(source, target, sems, do):
        for distance in range(1, SECTIONS):

            @pl.when(section + distance < SECTIONS)
            def _(distance=distance):
                do(remote(source, target.at[distance], sems, distance, {"section": section + distance}))

    def start(copy):
        copy.start()

    def sent(copy):
        copy.wait_send()

    pl.when(section < SECTIONS - 1)(lambda: pl.semaphore_wait(ready.at[1], SECTIONS - 1 - section))
    total = own_l
    for distance in ORDER:
        stay_copies[distance].wait_recv()
        total = total + recv_l[distance].astype(F32)
    delta_l[...] = total.astype(BF)
    later(delta_l, part_l, pl_sems, start)
    rows[...] = total
    total = own_m
    for distance in ORDER:
        come_copies[distance].wait_recv()
        total = total + recv_m[distance].astype(F32)
    delta_m[...] = total.astype(BF)
    later(delta_m, part_m, pm_sems, start)
    acc_m[...] = total

    for copy in tile_copies:
        copy.wait_recv()
    lens = jnp.zeros((8, 128), I32)
    plan = jnp.zeros((8, 128), I32)
    for slot in range(SLOTS):
        source = anchor[inst * SLOTS + slot] & (SLOTS - 1)
        lens = jnp.where(lane == slot, lengths[source], lens)
        plan = jnp.where(lane == slot, jnp.where(positions[slot] < 0, source, SLOTS + positions[slot]), plan)
    for at in range(len(SHIFTS)):
        for rank in range(MIG):
            value = jnp.sum(jnp.where(lane == rank, tile_in[at], 0), axis=1, keepdims=True)
            lens = jnp.where(lane == found[at * MIG + rank], value, lens)
    row = lax.broadcasted_iota(I32, (8, 128), 0)
    notes[...] = jnp.where(row == 0, lens, plan)

    for distance in range(1, SECTIONS):

        @pl.when(section >= distance)
        def _(distance=distance):
            remote(delta_l, part_l.at[distance], pl_sems, distance, {"section": section}).wait_recv()
            rows[...] += part_l[distance].astype(F32)

    small[4].wait()
    for distance in range(1, SECTIONS):

        @pl.when(section >= distance)
        def _(distance=distance):
            remote(delta_m, part_m.at[distance], pm_sems, distance, {"section": section}).wait_recv()
            acc_m[...] += part_m[distance].astype(F32)

    lines_l[0:8], lines_l[8:10] = unfold_stay(rows[...])
    lines_m[0:6] = unfold_come(acc_m[...])
    rank = jnp.int32(0)
    lines = []
    for slot in range(SLOTS):
        position = positions[slot]
        moved_row = lines_m[pl.ds(jnp.maximum(position, 0), 1), :]
        stay_row = lines_l[pl.ds(jnp.minimum(rank, STAY - 1), 1), :]
        lines.append(jnp.where(position >= 0, moved_row, stay_row))
        rank = rank + (position < 0).astype(I32)
    out[...] = (hidden[...].astype(F32) + jnp.concatenate(lines, axis=0)).astype(BF)

    later(delta_l, part_l, pl_sems, sent)
    later(delta_m, part_m, pm_sems, sent)
    for copy in list(stay_copies.values()) + list(come_copies.values()) + back_copies + tile_copies + ask_copies:
        copy.wait_send()
    for copy in early_copies + late_copies:
        copy.wait()


def place_kernel(kv_a, kv_b, early_in, late_in, out_rows, notes, out, moved, moved_len, plan, lens, sems):
    first = [
        pltpu.make_async_copy(notes, plan, sems.at[0]),
        pltpu.make_async_copy(out_rows, out.at[0], sems.at[1]),
    ]
    for copy in first:
        copy.start()
    first[0].wait()
    for slot in range(SLOTS):
        place = plan[1, slot]

        def move(low, high, cut, slot=slot):
            target = moved.at[0, slot, 0]
            pltpu.make_async_copy(low, target.at[pl.ds(0, cut)], sems.at[2]).start()
            pltpu.make_async_copy(high, target.at[pl.ds(cut, CTX - cut)], sems.at[2]).start()

        @pl.when(place < SLOTS)
        def _(place=place, move=move):
            move(kv_a.at[place], kv_b.at[place], EARLY)

        @pl.when(place >= SLOTS)
        def _(place=place, move=move):
            at, rank = lax.shift_right_logical(place - SLOTS, 1), place & 1
            move(early_in.at[at, rank], late_in.at[at, rank], EARLY)

    for slot in range(SLOTS):
        lens[slot] = plan[0, slot]
    last = pltpu.make_async_copy(lens, moved_len, sems.at[3])
    last.start()
    first[1].wait()
    pltpu.make_async_copy(moved, moved, sems.at[2]).wait()
    last.wait()


def specs(*spaces):
    return [pl.BlockSpec(memory_space=space) for space in spaces]


def body(hidden, queries, new_kv, kv_cache, lengths, anchor, out_weight):
    vmem, smem, hbm = pltpu.VMEM, pltpu.SMEM, pltpu.HBM
    dma = pltpu.SemaphoreType.DMA
    hidden, queries, new_kv, kv_cache, lengths, anchor, out_weight = (
        pltpu.with_memory_space_constraint(value, hbm)
        for value in (hidden, queries, new_kv, kv_cache, lengths, anchor, out_weight)
    )
    shapes = [
        ((SLOTS, EARLY, 2 * HD), BF), ((SLOTS, CTX - EARLY, 2 * HD), BF),
        ((3, MIG, EARLY, 2 * HD), BF), ((3, MIG, LATE, 2 * HD), BF),
        ((SLOTS, COLS), BF), ((8, 128), I32),
    ]
    made = pl.pallas_call(
        chain_kernel,
        out_shape=[vmem(*shape) for shape in shapes],
        in_specs=specs(*[hbm] * 7),
        out_specs=specs(*[vmem] * 6),
        scratch_shapes=[
            smem((INST * SLOTS,), I32), smem((SLOTS,), I32),
            vmem(queries.shape, BF), vmem(new_kv.shape, BF), vmem((SLOTS, COLS), BF),
            vmem((SLOTS, 8, HD), F32), vmem((SLOTS, 8, HD), F32),
            vmem((TP, GROUP * HD, COLS), BF),
            vmem((3, 16, HD), BF), vmem((3, 16, HD), BF),
            vmem((3, MIG, EARLY, 2 * HD), BF), vmem((3, MIG, LATE, 2 * HD), BF),
            vmem((3, 16, HD), BF), vmem((3, 16, HD), BF),
            vmem((3, 8, 128), I32), vmem((3, 8, 128), I32),
            vmem((8, 8, HD), F32),
            vmem((TP, 16, FOLD_L), BF), vmem((TP, 16, FOLD_L), BF),
            vmem((TP, 16, FOLD_M), BF), vmem((TP, 16, FOLD_M), BF),
            vmem((16, FOLD_L), BF), vmem((SECTIONS, 16, FOLD_L), BF),
            vmem((16, FOLD_M), BF), vmem((SECTIONS, 16, FOLD_M), BF),
            vmem((16, FOLD_L), F32), vmem((16, FOLD_M), F32),
            vmem((STAY, COLS), F32), vmem((MOVES, COLS), F32),
            dma((7,)), dma((TP,)), dma((2, 3)), dma((2, 3)), dma((2, 3)), dma((2, 3)), dma((2, 3)),
            dma((2, TP)), dma((2, TP)), dma((2, SECTIONS)), dma((2, SECTIONS)),
            pltpu.SemaphoreType.REGULAR((2,)),
        ],
        compiler_params=pltpu.CompilerParams(
            collective_id=0, has_side_effects=True, vmem_limit_bytes=32 << 20
        ),
        name="chain",
    )(anchor, lengths, queries, new_kv, hidden, kv_cache, out_weight)
    out, moved, moved_len = pl.pallas_call(
        place_kernel,
        out_shape=[
            jax.ShapeDtypeStruct((1, SLOTS, COLS), BF),
            jax.ShapeDtypeStruct(kv_cache.shape, BF),
            jax.ShapeDtypeStruct((SLOTS,), I32),
        ],
        in_specs=specs(*[vmem] * 6),
        out_specs=specs(hbm, hbm, hbm),
        scratch_shapes=[smem((8, 128), I32), smem((SLOTS,), I32), dma((4,))],
        compiler_params=pltpu.CompilerParams(vmem_limit_bytes=8 << 20),
        name="place",
    )(*made)
    return out, moved, moved_len


def solution(mesh):
    return jax.shard_map(
        body,
        mesh=mesh,
        in_specs=(
            P("inst", "tp"),
            P("section", "inst", "tp"),
            P("section", "inst", "tp"),
            P("section", "inst", "tp", None, None),
            P("inst"),
            P(),
            P("section", "tp", None),
        ),
        out_specs=(P("section", "inst", "tp"), P("section", "inst", "tp", None, None), P("inst")),
        check_vma=False,
    )
```

```python
import functools
import math

import jax
import jax.numpy as jnp
from jax import lax
from jax.experimental import pallas as pl
from jax.experimental.pallas import tpu as pltpu
from jax.sharding import PartitionSpec as P

MESH = pl.DeviceIdType.MESH
BF = jnp.bfloat16
F32 = jnp.float32
I32 = jnp.int32

INST = 4
TP = 8
SECTIONS = 8
SLOTS = 16
MIG = 2
GROUP = 4
HD = 128
CTX = 512
MODEL = 8192
COLS = MODEL // TP
FOLD_L = (SLOTS - 6) * COLS // 16
FOLD_M = 6 * COLS // 16
EARLY = 128
LATE = CTX - EARLY
SHIFTS = (1, 2, 3)
MOVES = len(SHIFTS) * MIG
STAY = SLOTS - MOVES
ORDER = (3, 5, 1, 7, 4, 2, 6)
INV_ROOT = 1.0 / math.sqrt(HD)

def wrap(value, count):
    return lax.rem(value + count, count)


def fold_stay(rows):
    step = COLS // 4
    tail = jnp.concatenate([rows[8:10, k * step : (k + 1) * step] for k in range(4)], axis=0)
    wide = jnp.concatenate([rows[:8], tail], axis=1)
    return jnp.concatenate([wide[:, :FOLD_L], wide[:, FOLD_L:]], axis=0)


def unfold_stay(folded):
    wide = jnp.concatenate([folded[:8], folded[8:]], axis=1)
    tail = jnp.concatenate([wide[2 * k : 2 * k + 2, COLS:] for k in range(4)], axis=1)
    return wide[:, :COLS], tail


def fold_come(rows):
    step = COLS // 4
    rest = [rows[k : k + 1, 3 * step :] for k in range(6)]
    wide = jnp.concatenate(
        [rows[:6, : 3 * step], jnp.concatenate(rest[:3], axis=1), jnp.concatenate(rest[3:], axis=1)], axis=0
    )
    return jnp.concatenate([wide[:, :FOLD_M], wide[:, FOLD_M:]], axis=0)


def unfold_come(folded):
    step = COLS // 4
    wide = jnp.concatenate([folded[:8], folded[8:]], axis=1)
    rest = [wide[6 + k // 3 : 7 + k // 3, (k % 3) * step : (k % 3 + 1) * step] for k in range(6)]
    return jnp.concatenate([wide[:6], jnp.concatenate(rest, axis=0)], axis=1)


def attend(queries, keys, values, lengths):
    scores = []
    for query, blocks in zip(queries, keys):
        rows = query.astype(BF)
        parts = [
            lax.dot_general(rows, block, (((1,), (1,)), ((), ())), preferred_element_type=F32) for block in blocks
        ]
        scores.append(jnp.concatenate(parts, axis=1))
    place = lax.broadcasted_iota(I32, (8, CTX), 1)
    probs = []
    for query, score, length in zip(queries, scores, lengths):
        score = jnp.where(place < length, score * INV_ROOT, -jnp.inf)
        new_score = jnp.sum(query * query[4:5, :], axis=1, keepdims=True) * INV_ROOT
        top = jnp.maximum(jnp.max(score, axis=1, keepdims=True), new_score)
        expo = jnp.exp(score - top)
        new_expo = jnp.exp(new_score - top)
        scale = 1.0 / (jnp.sum(expo, axis=1, keepdims=True) + new_expo)
        probs.append(((expo * scale).astype(BF), (new_expo * scale).astype(BF).astype(F32)))
    results = []
    for query, (prob, new_prob), blocks in zip(queries, probs, values):
        result = new_prob * query[5:6, :]
        start = 0
        for block in blocks:
            stop = start + block.shape[0]
            result = result + jnp.dot(prob[:, start:stop], block, preferred_element_type=F32)
            start = stop
        results.append(result)
    return results


def scan_leaving(anchor, me, shift):
    dest = wrap(me + shift, INST)
    count = jnp.int32(0)
    picked = [jnp.int32(0)] * MIG
    for slot in range(SLOTS):
        source = anchor[dest * SLOTS + slot]
        hit = lax.shift_right_logical(source, 4) == me
        for rank in range(MIG):
            picked[rank] = jnp.where(hit & (count == rank), source & (SLOTS - 1), picked[rank])
        count = count + hit.astype(I32)
    return picked


def scan_arriving(anchor, me):
    counts = [jnp.int32(0)] * len(SHIFTS)
    found = [jnp.int32(0)] * MOVES
    positions = []
    for slot in range(SLOTS):
        owner = lax.shift_right_logical(anchor[me * SLOTS + slot], 4)
        position = jnp.int32(-1)
        for at, shift in enumerate(SHIFTS):
            hit = owner == wrap(me - shift, INST)
            position = jnp.where(hit, at * MIG + jnp.minimum(counts[at], MIG - 1), position)
            for rank in range(MIG):
                one = at * MIG + rank
                found[one] = jnp.where(hit & (counts[at] == rank), slot, found[one])
            counts[at] = counts[at] + hit.astype(I32)
        positions.append(position)
    return positions, found


def scan_staying(anchor, me):
    rank = jnp.int32(0)
    slots = [jnp.int32(0)] * STAY
    for slot in range(SLOTS):
        hit = lax.shift_right_logical(anchor[me * SLOTS + slot], 4) == me
        for one in range(max(0, slot - MOVES), min(slot + 1, STAY)):
            slots[one] = jnp.where(hit & (rank == one), slot, slots[one])
        rank = rank + hit.astype(I32)
    return slots


def chain_kernel(
    anchor_in, lengths_in, q_in, new_in, hidden_in, kv, weight,
    kv_a, kv_b, early_in, late_in, out, notes,
    anchor, lengths, q_rows, new_rows, hidden, q_slots, table, w_blocks,
    asks, asks_in, early, late, back, back_in, tile, tile_in, rows_m,
    send_l, recv_l, send_m, recv_m, delta_l, part_l, delta_m, part_m, rows, acc_m, lines_l, lines_m,
    load_sems, w_sems, ask_sems, early_sems, back_sems, tile_sems, late_sems,
    l_sems, m_sems, pl_sems, pm_sems, ready,
):
    inst, section, tp = (lax.axis_index(name) for name in ("inst", "section", "tp"))
    far_half, row = lax.rem(tp, 2), lax.div(tp, 2)
    last = far_half * lax.div(row, TP // 2 - 1)

    def on_inst(shift):
        return {"inst": wrap(inst + shift, INST)}

    def on_tp(distance):
        return {"tp": wrap(tp + distance, TP)}

    def remote(source, target, sems, at, device):
        return pltpu.make_async_remote_copy(
            src_ref=source, dst_ref=target, send_sem=sems.at[0, at], recv_sem=sems.at[1, at],
            device_id=device, device_id_type=MESH,
        )

    def signal(sem, device):
        pl.semaphore_signal(sem, inc=1, device_id=device, device_id_type=MESH)

    barrier = pltpu.get_barrier_semaphore()
    for shift in SHIFTS:
        signal(barrier, on_inst(shift))
    small = [
        pltpu.make_async_copy(source, target, load_sems.at[at])
        for at, (source, target) in enumerate(
            (
                (anchor_in, anchor),
                (q_in, q_rows),
                (new_in, new_rows),
                (lengths_in, lengths),
                (hidden_in, hidden),
                (kv.at[0, :, 0, pl.ds(0, EARLY)], kv_a),
                (kv.at[0, :, 0, pl.ds(EARLY, CTX - EARLY)], kv_b),
            )
        )
    ]
    for copy in small:
        copy.start()
    for step in (1, 2, 3):
        pl.when(row + step < TP // 2)(lambda step=step: signal(barrier, {"tp": tp + 2 * step}))
    for step in range(1, SECTIONS):
        pl.when(section + step < SECTIONS)(lambda step=step: signal(barrier, {"section": section + step}))

    pl.when(far_half == 0)(lambda: signal(barrier, {"tp": TP - 1}))

    small[1].wait()
    small[2].wait()
    queries = q_rows[0].astype(F32)
    pairs = new_rows[0].astype(F32)
    for head in range(GROUP):
        q_slots[:, head, :] = queries[:, head * HD : (head + 1) * HD]
    q_slots[:, 4, :] = pairs[:, :HD]
    q_slots[:, 5, :] = pairs[:, HD:]
    q_slots[:, 6, :] = jnp.zeros((SLOTS, HD), F32)
    q_slots[:, 7, :] = jnp.zeros((SLOTS, HD), F32)
    small[0].wait()
    positions, found = scan_arriving(anchor, inst)
    for at in range(len(SHIFTS)):
        asks[at] = jnp.concatenate([q_slots[found[at * MIG + rank]] for rank in range(MIG)], axis=0).astype(BF)
    leaving = [scan_leaving(anchor, inst, shift) for shift in SHIFTS]

    small[5].wait()
    early_copies, late_copies, back_copies, tile_copies = [], [], [], []
    for at, shift in enumerate(SHIFTS):
        early_copies.append(remote(early.at[at], early_in.at[at], early_sems, at, on_inst(shift)))
        late_copies.append(remote(late.at[at], late_in.at[at], late_sems, at, on_inst(shift)))
        back_copies.append(remote(back.at[at], back_in.at[at], back_sems, at, on_inst(shift)))
        tile_copies.append(remote(tile.at[at], tile_in.at[at], tile_sems, at, on_inst(shift)))
    for at in range(len(SHIFTS)):
        for rank in range(MIG):
            early[at, rank] = kv_a[leaving[at][rank]]
    small[3].wait()
    lane = lax.broadcasted_iota(I32, (8, 128), 1)
    for at in range(len(SHIFTS)):
        filled = jnp.zeros((8, 128), I32)
        for rank in range(MIG):
            filled = jnp.where(lane == rank, lengths[leaving[at][rank]], filled)
        tile[at] = filled
    pl.semaphore_wait(barrier, len(SHIFTS) + row + section + last * (TP // 2))
    ask_copies = [
        remote(asks.at[at], asks_in.at[at], ask_sems, at, on_inst(-shift)) for at, shift in enumerate(SHIFTS)
    ]
    for copy in ask_copies:
        copy.start()

    for at in (1, 0, 2):
        early_copies[at].start()
    for copy in tile_copies:
        copy.start()

    @pl.when(last == 1)
    def _():
        for step in range(TP // 2):
            signal(ready.at[0], {"tp": 2 * step})

    for step in (1, 2, 3):
        pl.when(row >= step)(lambda step=step: signal(ready.at[0], {"tp": tp - 2 * step}))
    for step in range(1, SECTIONS):
        pl.when(section >= step)(lambda step=step: signal(ready.at[1], {"section": section - step}))

    small[6].wait()
    loads = {}
    for distance in ORDER + (0,):
        columns = pl.ds(pl.multiple_of(wrap(tp + distance, TP) * COLS, COLS), COLS)
        loads[distance] = pltpu.make_async_copy(
            weight.at[0, :, columns], w_blocks.at[distance], w_sems.at[distance]
        )
        loads[distance].start()
    for at in range(len(SHIFTS)):
        for rank in range(MIG):
            slot = leaving[at][rank]
            late[at, rank] = kv_b[slot]

    def attend_at(queries, slots):
        return attend(
            queries,
            [[kv_a[slot, :, :HD], kv_b[slot, :, :HD]] for slot in slots],
            [[kv_a[slot, :, HD:], kv_b[slot, :, HD:]] for slot in slots],
            [lengths[slot] for slot in slots],
        )

    staying = scan_staying(anchor, inst)
    sources = [anchor[inst * SLOTS + slot] & (SLOTS - 1) for slot in staying]
    for one, result in enumerate(attend_at([q_slots[slot] for slot in staying], sources)):
        table[one] = result

    asked = []
    for at in range(len(SHIFTS)):
        ask_copies[at].wait_recv()
        both = asks_in[at].astype(F32)
        asked += [both[rank * 8 : rank * 8 + 8, :] for rank in range(MIG)]
    results = attend_at(asked, [slot for pair in leaving for slot in pair])
    for at in range(len(SHIFTS)):
        back[at] = jnp.concatenate(results[at * MIG : at * MIG + MIG], axis=0).astype(BF)
        back_copies[at].start()
    for at in (1, 0, 2):
        late_copies[at].start()

    for one in range(STAY, SLOTS):
        table[one] = jnp.zeros((8, HD), F32)
    stay = jnp.concatenate([table[:, head, :] for head in range(GROUP)], axis=1).astype(BF)

    unheard = TP // 2 - 1 - row + 1 - far_half
    pl.when(unheard > 0)(lambda: pl.semaphore_wait(ready.at[0], unheard))

    stay_copies = {}
    own_l = None
    for distance in ORDER + (0,):
        loads[distance].wait()
        share = fold_stay(jnp.dot(stay, w_blocks[distance], preferred_element_type=F32))
        if distance == 0:
            own_l = share
        else:
            send_l[distance] = share.astype(BF)
            copy = remote(send_l.at[distance], recv_l.at[distance], l_sems, distance, on_tp(distance))
            copy.start()
            stay_copies[distance] = copy

    for copy in back_copies:
        copy.wait_recv()
    for at in range(len(SHIFTS)):
        both = back_in[at].astype(F32)
        for rank in range(MIG):
            rows_m[at * MIG + rank] = both[rank * 8 : rank * 8 + 8, :]
    rows_m[6] = jnp.zeros((8, HD), F32)
    rows_m[7] = jnp.zeros((8, HD), F32)
    come = jnp.concatenate([rows_m[:, head, :] for head in range(GROUP)], axis=1).astype(BF)
    come_copies = {}
    own_m = None
    for distance in ORDER + (0,):
        share = fold_come(jnp.dot(come, w_blocks[distance], preferred_element_type=F32))
        if distance == 0:
            own_m = share
        else:
            send_m[distance] = share.astype(BF)
            copy = remote(send_m.at[distance], recv_m.at[distance], m_sems, distance, on_tp(distance))
            copy.start()
            come_copies[distance] = copy

    def later(source, target, sems, do):
        for distance in range(1, SECTIONS):

            @pl.when(section + distance < SECTIONS)
            def _(distance=distance):
                do(remote(source, target.at[distance], sems, distance, {"section": section + distance}))

    def start(copy):
        copy.start()

    def sent(copy):
        copy.wait_send()

    pl.when(section < SECTIONS - 1)(lambda: pl.semaphore_wait(ready.at[1], SECTIONS - 1 - section))
    total = own_l
    for distance in ORDER:
        stay_copies[distance].wait_recv()
        total = total + recv_l[distance].astype(F32)
    delta_l[...] = total.astype(BF)
    later(delta_l, part_l, pl_sems, start)
    rows[...] = total
    total = own_m
    for distance in ORDER:
        come_copies[distance].wait_recv()
        total = total + recv_m[distance].astype(F32)
    delta_m[...] = total.astype(BF)
    later(delta_m, part_m, pm_sems, start)
    acc_m[...] = total

    for copy in tile_copies:
        copy.wait_recv()
    lens = jnp.zeros((8, 128), I32)
    plan = jnp.zeros((8, 128), I32)
    for slot in range(SLOTS):
        source = anchor[inst * SLOTS + slot] & (SLOTS - 1)
        lens = jnp.where(lane == slot, lengths[source], lens)
        plan = jnp.where(lane == slot, jnp.where(positions[slot] < 0, source, SLOTS + positions[slot]), plan)
    for at in range(len(SHIFTS)):
        for rank in range(MIG):
            value = jnp.sum(jnp.where(lane == rank, tile_in[at], 0), axis=1, keepdims=True)
            lens = jnp.where(lane == found[at * MIG + rank], value, lens)
    row = lax.broadcasted_iota(I32, (8, 128), 0)
    notes[...] = jnp.where(row == 0, lens, plan)

    for distance in range(1, SECTIONS):

        @pl.when(section >= distance)
        def _(distance=distance):
            remote(delta_l, part_l.at[distance], pl_sems, distance, {"section": section}).wait_recv()
            rows[...] += part_l[distance].astype(F32)

    small[4].wait()
    for distance in range(1, SECTIONS):

        @pl.when(section >= distance)
        def _(distance=distance):
            remote(delta_m, part_m.at[distance], pm_sems, distance, {"section": section}).wait_recv()
            acc_m[...] += part_m[distance].astype(F32)

    lines_l[0:8], lines_l[8:10] = unfold_stay(rows[...])
    lines_m[0:6] = unfold_come(acc_m[...])
    rank = jnp.int32(0)
    lines = []
    for slot in range(SLOTS):
        position = positions[slot]
        moved_row = lines_m[pl.ds(jnp.maximum(position, 0), 1), :]
        stay_row = lines_l[pl.ds(jnp.minimum(rank, STAY - 1), 1), :]
        lines.append(jnp.where(position >= 0, moved_row, stay_row))
        rank = rank + (position < 0).astype(I32)
    out[...] = (hidden[...].astype(F32) + jnp.concatenate(lines, axis=0)).astype(BF)

    later(delta_l, part_l, pl_sems, sent)
    later(delta_m, part_m, pm_sems, sent)
    for copy in list(stay_copies.values()) + list(come_copies.values()) + back_copies + tile_copies + ask_copies:
        copy.wait_send()
    for copy in early_copies + late_copies:
        copy.wait()


def place_kernel(kv_a, kv_b, early_in, late_in, out_rows, notes, out, moved, moved_len, plan, lens, sems):
    first = [
        pltpu.make_async_copy(notes, plan, sems.at[0]),
        pltpu.make_async_copy(out_rows, out.at[0], sems.at[1]),
    ]
    for copy in first:
        copy.start()
    first[0].wait()
    for slot in range(SLOTS):
        place = plan[1, slot]

        def move(low, high, cut, slot=slot):
            target = moved.at[0, slot, 0]
            pltpu.make_async_copy(low, target.at[pl.ds(0, cut)], sems.at[2]).start()
            pltpu.make_async_copy(high, target.at[pl.ds(cut, CTX - cut)], sems.at[2]).start()

        @pl.when(place < SLOTS)
        def _(place=place, move=move):
            move(kv_a.at[place], kv_b.at[place], EARLY)

        @pl.when(place >= SLOTS)
        def _(place=place, move=move):
            at, rank = lax.shift_right_logical(place - SLOTS, 1), place & 1
            move(early_in.at[at, rank], late_in.at[at, rank], EARLY)

    for slot in range(SLOTS):
        lens[slot] = plan[0, slot]
    last = pltpu.make_async_copy(lens, moved_len, sems.at[3])
    last.start()
    first[1].wait()
    pltpu.make_async_copy(moved, moved, sems.at[2]).wait()
    last.wait()


def specs(*spaces):
    return [pl.BlockSpec(memory_space=space) for space in spaces]


def body(hidden, queries, new_kv, kv_cache, lengths, anchor, out_weight):
    vmem, smem, hbm = pltpu.VMEM, pltpu.SMEM, pltpu.HBM
    dma = pltpu.SemaphoreType.DMA
    hidden, queries, new_kv, kv_cache, lengths, anchor, out_weight = (
        pltpu.with_memory_space_constraint(value, hbm)
        for value in (hidden, queries, new_kv, kv_cache, lengths, anchor, out_weight)
    )
    shapes = [
        ((SLOTS, EARLY, 2 * HD), BF), ((SLOTS, CTX - EARLY, 2 * HD), BF),
        ((3, MIG, EARLY, 2 * HD), BF), ((3, MIG, LATE, 2 * HD), BF),
        ((SLOTS, COLS), BF), ((8, 128), I32),
    ]
    made = pl.pallas_call(
        chain_kernel,
        out_shape=[vmem(*shape) for shape in shapes],
        in_specs=specs(*[hbm] * 7),
        out_specs=specs(*[vmem] * 6),
        scratch_shapes=[
            smem((INST * SLOTS,), I32), smem((SLOTS,), I32),
            vmem(queries.shape, BF), vmem(new_kv.shape, BF), vmem((SLOTS, COLS), BF),
            vmem((SLOTS, 8, HD), F32), vmem((SLOTS, 8, HD), F32),
            vmem((TP, GROUP * HD, COLS), BF),
            vmem((3, 16, HD), BF), vmem((3, 16, HD), BF),
            vmem((3, MIG, EARLY, 2 * HD), BF), vmem((3, MIG, LATE, 2 * HD), BF),
            vmem((3, 16, HD), BF), vmem((3, 16, HD), BF),
            vmem((3, 8, 128), I32), vmem((3, 8, 128), I32),
            vmem((8, 8, HD), F32),
            vmem((TP, 16, FOLD_L), BF), vmem((TP, 16, FOLD_L), BF),
            vmem((TP, 16, FOLD_M), BF), vmem((TP, 16, FOLD_M), BF),
            vmem((16, FOLD_L), BF), vmem((SECTIONS, 16, FOLD_L), BF),
            vmem((16, FOLD_M), BF), vmem((SECTIONS, 16, FOLD_M), BF),
            vmem((16, FOLD_L), F32), vmem((16, FOLD_M), F32),
            vmem((STAY, COLS), F32), vmem((MOVES, COLS), F32),
            dma((7,)), dma((TP,)), dma((2, 3)), dma((2, 3)), dma((2, 3)), dma((2, 3)), dma((2, 3)),
            dma((2, TP)), dma((2, TP)), dma((2, SECTIONS)), dma((2, SECTIONS)),
            pltpu.SemaphoreType.REGULAR((2,)),
        ],
        compiler_params=pltpu.CompilerParams(
            collective_id=0, has_side_effects=True, vmem_limit_bytes=32 << 20
        ),
        name="chain",
    )(anchor, lengths, queries, new_kv, hidden, kv_cache, out_weight)
    out, moved, moved_len = pl.pallas_call(
        place_kernel,
        out_shape=[
            jax.ShapeDtypeStruct((1, SLOTS, COLS), BF),
            jax.ShapeDtypeStruct(kv_cache.shape, BF),
            jax.ShapeDtypeStruct((SLOTS,), I32),
        ],
        in_specs=specs(*[vmem] * 6),
        out_specs=specs(hbm, hbm, hbm),
        scratch_shapes=[smem((8, 128), I32), smem((SLOTS,), I32), dma((4,))],
        compiler_params=pltpu.CompilerParams(vmem_limit_bytes=8 << 20),
        name="place",
    )(*made)
    return out, moved, moved_len


def solution(mesh):
    return jax.shard_map(
        body,
        mesh=mesh,
        in_specs=(
            P("inst", "tp"),
            P("section", "inst", "tp"),
            P("section", "inst", "tp"),
            P("section", "inst", "tp", None, None),
            P("inst"),
            P(),
            P("section", "tp", None),
        ),
        out_specs=(P("section", "inst", "tp"), P("section", "inst", "tp", None, None), P("inst")),
        check_vma=False,
    )
```
